256 devices in a mesh: ctx: 16 (over x, y), fsdp: 16 (over z, core).
Axes of the slice: x: 4, y: 4, z: 8, core: 2. Of those that a mesh axis runs over, the one named last changes fastest.
Arguments:
- hidden: bfloat16 [16, 7168, 5120], P('fsdp', 'ctx'), may hold values from -6 to 6
- modulation: float32 [2, 5120], replicated, may hold values from -3 to 3
- head_weight: bfloat16 [64, 5120], replicated, may hold values from -0.078125 to 0.078125
- noisy: bfloat16 [16, 7168, 64], P('fsdp', 'ctx'), may hold values from -6 to 6
- timestep: int32 [1], replicated, may hold values from 1 to 999
- conv_weight: bfloat16 [3, 64, 384], replicated, may hold values from -0.4375 to 0.4375
- up_weight: bfloat16 [4, 384, 384], replicated, may hold values from -0.3125 to 0.3125
- patch_proj: bfloat16 [384, 1280], replicated, may hold values from -0.3125 to 0.3125
- fc1: bfloat16 [1280, 5120], P(None, 'fsdp'), may hold values from -0.15625 to 0.15625
- reward_vec: bfloat16 [1, 5120], P(None, 'fsdp'), may hold values from -0.078125 to 0.078125
Outputs:
- grad_hidden: bfloat16 [16, 7168, 5120], P('fsdp', 'ctx')
- rewards: float32 [16, 128], P('fsdp', 'ctx')
The draws below stay inside these ranges and needn't reach their ends.
All inputs are finite; a program needn't handle non-finite values.
Results may differ from the reference program's by a relative error of at most 0.024.
Values may be sent and summed in bfloat16 or wider, within the bound.
A program may use at most 128 MiB of HBM per device.

```python
import jax
import jax.numpy as jnp
from jax import lax

D = 5120
DECODER_CHANNELS = 384
R = 1280
F4 = 5120
PATCH = 64
POOLED_REGIONS = 4
TPF = 224
LF = 32
FRAME_SLOTS = 128
TOKENS = 7168
VIDEOS = 16


def block_scale(key, extent, cuts, smallest, high):
    loudness, own = 1.0, jax.random.fold_in(key, 6)
    for dim, parts in cuts:
        steps = jnp.exp(jax.random.uniform(jax.random.fold_in(own, dim), (parts,), jnp.float32, smallest / len(cuts), high / len(cuts)))
        loudness = loudness * jnp.repeat(steps, extent[dim] // parts).reshape([-1 if axis == dim else 1 for axis in range(len(extent))])
    return loudness


def centred(key, dims, scale, reach, pieces=(), dtype=jnp.bfloat16):
    drawn = jax.random.normal(key, dims, jnp.float32) * scale
    if len(pieces) > 0:
        drawn = block_scale(key, dims, pieces, -0.22, 0.18) * drawn
    return jnp.clip(drawn, min=-reach, max=reach).astype(dtype)


def setup_inputs(seed: int = 0) -> dict:
    keys = jax.random.split(jax.random.key(seed), 11)
    return {
        "hidden": centred(keys[0], (VIDEOS, TOKENS, D), 1.0, 6.0, ((0, 16), (1, 16))),
        "modulation": centred(keys[1], (2, D), 0.5, 3.0, (), jnp.float32),
        "head_weight": centred(keys[2], (PATCH, D), D ** -0.5, 0.078125),
        "noisy": centred(keys[3], (VIDEOS, TOKENS, PATCH), 1.0, 6.0, ((0, 16), (1, 16))),
        "timestep": jax.random.randint(keys[4], (1,), 1, 1000).astype(jnp.int32),
        "conv_weight": centred(keys[5], (3, PATCH, DECODER_CHANNELS), (3 * PATCH) ** -0.5, 0.4375),
        "up_weight": centred(keys[6], (4, DECODER_CHANNELS, DECODER_CHANNELS), DECODER_CHANNELS ** -0.5, 0.3125),
        "patch_proj": centred(keys[7], (DECODER_CHANNELS, R), DECODER_CHANNELS ** -0.5, 0.3125),
        "fc1": centred(keys[8], (R, F4), R ** -0.5, 0.15625, ((1, 16),)),
        "reward_vec": centred(keys[9], (1, F4), F4 ** -0.5, 0.078125, ((1, 16),)),
    }


LOSS_WEIGHT = 65536.0
EPSILON = 1e-06

def gelu_slope(value):
    coeff = 0.7978845608028654
    inner = coeff * (value + 0.044715 * value * value * value)
    tangent = jnp.tanh(inner)
    return 0.5 * (1.0 + tangent) + 0.5 * value * (1.0 - tangent * tangent) * coeff * (1.0 + 3.0 * 0.044715 * value * value)

def silu_slope(value):
    sig = jax.nn.sigmoid(value)
    return sig * (1.0 + value * (1.0 - sig))

def normalize(value):
    center = value - lax.optimization_barrier(jnp.mean(value, axis=-1, keepdims=True))
    scale = lax.rsqrt(lax.optimization_barrier(jnp.mean(center * center, axis=-1, keepdims=True)) + EPSILON)
    return (center * scale, scale)

def norm_back(grad, normed, scale):
    return (grad - lax.optimization_barrier(jnp.mean(grad, axis=-1, keepdims=True)) - normed * lax.optimization_barrier(jnp.mean(grad * normed, axis=-1, keepdims=True))) * scale

def reference(hidden, modulation, head_weight, noisy, timestep, conv_weight, up_weight, patch_proj, fc1, reward_vec):
    step_frac = timestep[0].astype(jnp.float32) / 1000.0
    sigma = 5.0 * step_frac / (1.0 + 4.0 * step_frac)
    slot_index = jnp.arange(FRAME_SLOTS)
    slot_present = ((slot_index == 0) | (slot_index >= 4)).astype(jnp.float32)
    vec32 = reward_vec[0].astype(jnp.float32)
    conv32 = conv_weight.astype(jnp.float32)
    up32 = up_weight.astype(jnp.float32)

    def one_video(pair):
        states, latents = pair
        normed, scale = normalize(states.astype(jnp.float32))
        modded = (normed * (1.0 + modulation[1]) + modulation[0]).astype(jnp.bfloat16)
        vel = jnp.dot(modded, head_weight.T, preferred_element_type=jnp.float32)
        x0 = (latents.astype(jnp.float32) - sigma * vel).astype(jnp.bfloat16).reshape(LF, TPF, PATCH)
        ext = jnp.concatenate([jnp.zeros((2, TPF, PATCH), jnp.bfloat16), x0], axis=0).astype(jnp.float32)
        a0 = sum((jnp.einsum('ftp,pc->ftc', ext[2 - k:2 - k + LF], conv32[k]) for k in range(3)))
        feat = jax.nn.silu(a0).astype(jnp.bfloat16).astype(jnp.float32)
        a1 = jnp.einsum('ftc,jcd->fjtd', feat, up32)
        embedding_rows = lax.optimization_barrier(jnp.mean(jax.nn.silu(a1).reshape(LF, 4, POOLED_REGIONS, TPF // POOLED_REGIONS, DECODER_CHANNELS), axis=3))
        embedding_rows = embedding_rows.astype(jnp.bfloat16).reshape(FRAME_SLOTS * POOLED_REGIONS, DECODER_CHANNELS)
        u = jnp.dot(embedding_rows, patch_proj, preferred_element_type=jnp.float32)
        nhat, uscale = normalize(u)
        n = nhat.astype(jnp.bfloat16)
        m = jnp.dot(n, fc1, preferred_element_type=jnp.float32)
        reward_score = lax.optimization_barrier(jnp.sum(jax.nn.gelu(m, approximate=True) * vec32, axis=-1))
        rewards = lax.optimization_barrier(jnp.mean(reward_score.reshape(FRAME_SLOTS, POOLED_REGIONS), axis=1)) * slot_present
        row_scale = jnp.repeat(-LOSS_WEIGHT * slot_present / POOLED_REGIONS, POOLED_REGIONS)
        g = (vec32 * gelu_slope(m)).astype(jnp.bfloat16)
        dn = jnp.dot(g, fc1.T, preferred_element_type=jnp.float32) * row_scale[:, None]
        du = norm_back(dn, nhat, uscale).astype(jnp.bfloat16)
        demb = jnp.dot(du, patch_proj.T, preferred_element_type=jnp.float32).reshape(LF, 4, POOLED_REGIONS, 1, DECODER_CHANNELS)
        spread = jnp.broadcast_to(demb, (LF, 4, POOLED_REGIONS, TPF // POOLED_REGIONS, DECODER_CHANNELS)).reshape(LF, 4, TPF, DECODER_CHANNELS)
        da1 = (spread / (TPF // POOLED_REGIONS) * silu_slope(a1)).astype(jnp.bfloat16).astype(jnp.float32)
        dfeat = jnp.einsum('fjtd,jcd->ftc', da1, up32)
        da0 = (dfeat * silu_slope(a0)).astype(jnp.bfloat16)
        extd = jnp.concatenate([da0, jnp.zeros((2, TPF, DECODER_CHANNELS), jnp.bfloat16)], axis=0).astype(jnp.float32)
        dx0 = sum((jnp.einsum('ftc,pc->ftp', extd[k:k + LF], conv32[k]) for k in range(3)))
        dvel = (-sigma * dx0).astype(jnp.bfloat16).reshape(TOKENS, PATCH)
        dmod = jnp.dot(dvel, head_weight, preferred_element_type=jnp.float32)
        dnormed = dmod * (1.0 + modulation[1])
        grad = norm_back(dnormed, normed, scale).astype(jnp.bfloat16)
        return (grad, rewards)
    grads, rewards = lax.map(one_video, (hidden, noisy))
    return (grads, rewards)
```

```python
import jax
import jax.numpy as jnp
from jax import lax
from jax.experimental import pallas as pl
from jax.experimental.pallas import tpu as pltpu
from jax.sharding import PartitionSpec as P

TPF = 224
REGIONS = 4
SUB = 4
LOSS_WEIGHT = 65536.0
EPSILON = 1e-06
F32 = jnp.float32
BF16 = jnp.bfloat16
MESH = pl.DeviceIdType.MESH


def dot_nn(a, b):
    return lax.dot_general(a, b, (((1,), (0,)), ((), ())), preferred_element_type=F32)


def dot_nt(a, b):
    return lax.dot_general(a, b, (((1,), (1,)), ((), ())), preferred_element_type=F32)


def sigmoid(value):
    return 0.5 + 0.5 * jnp.tanh(0.5 * value)


def main_kernel(
    timestep,
    hidden,
    modulation,
    head_weight,
    noisy_t,
    conv_weight,
    up_weight,
    patch_proj,
    fc1_t,
    reward_vec,
    lhs_out,
    coef_out,
    reward_out,
    hid,
    mod,
    head,
    noisy,
    conv,
    up,
    proj,
    cols,
    vec,
    vec_in,
    acc,
    aux,
    ssq,
    pilot,
    vel0,
    rstd,
    mean,
    xown,
    xhalo,
    a0,
    feat,
    a1,
    emb32,
    eall,
    u,
    uscale,
    n,
    g,
    dn,
    du,
    dsend,
    drecv,
    ssend,
    srecv,
    da1,
    da0,
    hsend,
    hrecv,
    hid_sem,
    in_sem,
    far_send,
    far_recv,
    emb_send,
    emb_recv,
    dem_send,
    dem_recv,
    sco_send,
    sco_recv,
):
    chunks, tokens, width = hid.shape
    full = chunks * width
    patch = head.shape[0]
    channels = proj.shape[0]
    shard = fc1_t.shape[0]
    span = TPF // REGIONS
    rows = eall.shape[1]
    spots = eall.shape[0]

    ctx, fsdp = lax.axis_index("ctx"), lax.axis_index("fsdp")
    steps, flat = lax.axis_size("ctx"), lax.axis_size("fsdp")
    z, core = fsdp // 2, fsdp % 2
    after = (lax.rem(ctx + 1, steps), fsdp)
    before = (lax.rem(ctx + steps - 1, steps), fsdp)
    twin = (ctx, z * 2 + 1 - core)
    ups = [None] + [(ctx, lax.rem(z + d, spots) * 2 + core) for d in range(1, spots)]
    downs = [None] + [(ctx, lax.rem(z + spots - d, spots) * 2 + core) for d in range(1, spots)]

    loads = []

    def load(source, target):
        copy = pltpu.make_async_copy(source, target, in_sem.at[len(loads)])
        copy.start()
        loads.append(copy)
        return copy

    hid_loads = []

    def load_hidden(k):
        copy = pltpu.make_async_copy(
            hidden.at[:, pl.ds(k * width, width)], hid.at[k], hid_sem.at[k]
        )
        copy.start()
        hid_loads.append(copy)

    load_mod = load(modulation, mod)
    load_head = load(head_weight, head)
    for k in range(chunks):
        load_hidden(k)

    barrier = pltpu.get_barrier_semaphore()
    peers = [after, before, twin] + ups[1:]
    for peer in peers:
        pl.semaphore_signal(barrier, inc=1, device_id=peer, device_id_type=MESH)

    load_noisy = load(noisy_t, noisy)
    load_conv = []
    for frame in range(2):
        for lag in range(3):
            block = frame + 2 - lag
            load_conv.append(
                load(
                    conv_weight.at[lag],
                    conv.at[pl.ds(block * patch, patch), pl.ds(frame * channels, channels)],
                )
            )
    load_up = [
        load(up_weight.at[j], up.at[:, pl.ds(j * channels, channels)]) for j in range(SUB)
    ]
    load_proj = load(patch_proj, proj)
    load_cols = load(fc1_t, cols.at[pl.ds(0, shard)])
    load_vec = load(reward_vec, vec_in)

    empty = jnp.zeros((patch, channels), BF16)
    conv[0:patch, channels:] = empty
    conv[3 * patch :, :channels] = empty

    step_frac = jnp.full((1, 2 * patch), timestep[0].astype(F32)) / 1000.0
    sigma = 5.0 * step_frac / (1.0 + 4.0 * step_frac)
    left = lax.broadcasted_iota(jnp.int32, (TPF, 2 * patch), 1) < patch

    load_mod.wait()
    load_head.wait()
    hid_loads[0].wait()
    pilot[...] = jnp.broadcast_to(hid[0, :, 0:1].astype(F32), pilot.shape)
    acc[...] = jnp.zeros_like(acc)
    aux[...] = jnp.zeros_like(aux)
    ssq[...] = jnp.zeros_like(ssq)
    lanes = pilot.shape[1]
    block_rows = 16

    def features(k, carry):
        columns = pl.ds(pl.multiple_of(k * width, width), width)
        shift = mod[0:1, columns]
        high = shift.astype(BF16)
        low = (shift - high.astype(F32)).astype(BF16)
        side = jnp.concatenate(
            [
                jnp.ones((8, width), F32),
                jnp.broadcast_to(high.astype(F32), (8, width)),
                jnp.broadcast_to(low.astype(F32), (8, width)),
                jnp.zeros((8, width), F32),
            ],
            axis=0,
        ).astype(BF16)
        plain = head[:, columns]
        scaled = (plain.astype(F32) * (1.0 + mod[1:2, columns])).astype(BF16)
        ones = jnp.ones((patch, width), BF16)
        acc[...] += dot_nt(hid[k], jnp.concatenate([scaled, ones], axis=0))
        aux[...] += dot_nt(side, jnp.concatenate([scaled, plain], axis=0))
        for r in range(0, tokens, block_rows):
            centre = pilot[r : r + block_rows, :]
            total = ssq[r : r + block_rows, :]
            for c in range(0, width, lanes):
                value = hid[k, r : r + block_rows, c : c + lanes].astype(F32) - centre
                total = total + value * value
            ssq[r : r + block_rows, :] = total
        return carry

    features(0, 0)

    def later(k, carry):
        pltpu.make_async_copy(hid.at[k], hid.at[k], hid_sem.at[k]).wait()
        return features(k, carry)

    lax.fori_loop(1, chunks, later, 0)

    load_noisy.wait()
    pair = noisy[...]
    pair = jnp.concatenate([pair, pair], axis=0)
    row_id = lax.broadcasted_iota(jnp.int32, (TPF, 2 * TPF), 0)
    col_id = lax.broadcasted_iota(jnp.int32, (TPF, 2 * TPF), 1)
    first = dot_nt((row_id == col_id).astype(F32).astype(BF16), pair)
    second = dot_nt((row_id + TPF == col_id).astype(F32).astype(BF16), pair)
    latents = jnp.where(left, first, second)

    side_left = lax.broadcasted_iota(jnp.int32, (1, 2 * patch), 1) < patch
    sums = aux[0:1, :]
    shifts = aux[8:9, :] + aux[16:17, :]
    head_sums = jnp.where(side_left, sums, pltpu.roll(sums, patch, 1))
    head_shift = jnp.where(side_left, pltpu.roll(shifts, patch, 1), shifts)
    means, stds = [], []
    for f in range(2):
        part = slice(f * TPF, (f + 1) * TPF)
        average = acc[part, patch : patch + 1] / full
        off = average - pilot[part, 0:1]
        square = jnp.sum(ssq[part, :], axis=1, keepdims=True) / full
        var = jnp.maximum(square - off * off, 0.0)
        means.append(jnp.broadcast_to(average, (TPF, 2 * patch)))
        stds.append(jnp.broadcast_to(lax.rsqrt(var + EPSILON), (TPF, 2 * patch)))
    mean[...] = jnp.where(left, means[0], means[1])
    rstd[...] = jnp.where(left, stds[0], stds[1])
    product = jnp.where(left, acc[0:TPF, :], pltpu.roll(acc[TPF:, :], patch, 1))
    vel0[...] = rstd[...] * (product - mean[...] * head_sums)
    xown[...] = (latents - sigma * (vel0[...] + head_shift)).astype(BF16)

    pl.semaphore_wait(barrier, len(peers))

    def far(source, target, index, device):
        copy = pltpu.make_async_remote_copy(
            src_ref=source,
            dst_ref=target,
            send_sem=far_send.at[index],
            recv_sem=far_recv.at[index],
            device_id=device,
            device_id_type=MESH,
        )
        copy.start()
        return copy

    move_x = far(xown, xhalo, 0, after)
    move_cols = far(fc1_t, cols.at[pl.ds(shard, shard)], 1, twin)
    load_vec.wait()
    vec[0] = jnp.broadcast_to(vec_in[...].astype(F32), vec.shape[1:])
    move_vec = far(vec.at[0], vec.at[1], 2, twin)

    for copy in load_conv:
        copy.wait()
    a0[...] = dot_nn(xown[...], conv[2 * patch :, :])
    for copy in load_up:
        copy.wait()
    move_x.wait_recv()
    live_before = jnp.where(ctx > 0, 1.0, 0.0)
    halo = (xhalo[...].astype(F32) * live_before).astype(BF16)
    a0[...] += dot_nn(halo, conv[0 : 2 * patch, :])
    for f in range(2):
        value = a0[:, f * channels : (f + 1) * channels]
        feat[f * TPF : (f + 1) * TPF, :] = (value * sigmoid(value)).astype(BF16)

    for j in range(SUB):
        part = slice(j * channels, (j + 1) * channels)
        a1[:, part] = dot_nn(feat[...], up[:, part])
        for f in range(2):
            for p in range(REGIONS):
                begin = f * TPF + p * span
                value = a1[begin : begin + span, part]
                pooled = jnp.sum(value * sigmoid(value), axis=0, keepdims=True) / span
                row = p * 2 * SUB + f * SUB + j
                emb32[row : row + 1, :] = pooled
    eall[0] = emb32[...].astype(BF16)

    order = sorted(range(1, spots), key=lambda d: (-min(d, spots - d), d))
    move_emb = []
    for d in order:
        copy = pltpu.make_async_remote_copy(
            src_ref=eall.at[0],
            dst_ref=eall.at[d],
            send_sem=emb_send.at[d],
            recv_sem=emb_recv.at[d],
            device_id=ups[d],
            device_id_type=MESH,
        )
        copy.start()
        move_emb.append(copy)

    for f in range(2):
        for p in range(REGIONS):
            begin = f * TPF + p * span
            for j in range(SUB):
                part = slice(j * channels, (j + 1) * channels)
                value = a1[begin : begin + span, part]
                gate = sigmoid(value)
                a1[begin : begin + span, part] = gate * (1.0 + value * (1.0 - gate))
        part = slice(f * channels, (f + 1) * channels)
        value = a0[:, part]
        gate = sigmoid(value)
        a0[:, part] = gate * (1.0 + value * (1.0 - gate))

    load_proj.wait()
    load_cols.wait()
    move_cols.wait_recv()
    move_vec.wait_recv()
    for copy in move_emb:
        copy.wait_recv()

    features_r = proj.shape[1]
    stacked = jnp.concatenate([eall[d] for d in range(spots)], axis=0)
    u[...] = dot_nn(stacked, proj[...])
    for d in range(spots):
        part = slice(d * rows, (d + 1) * rows)
        value = u[part, :]
        centre = value - jnp.mean(value, axis=-1, keepdims=True)
        scale = lax.rsqrt(jnp.mean(centre * centre, axis=-1, keepdims=True) + EPSILON)
        normed = centre * scale
        u[part, :] = normed
        uscale[part, :] = jnp.broadcast_to(scale, (rows, uscale.shape[1]))
        n[part, :] = normed.astype(BF16)
    weight = jnp.concatenate([vec[0], vec[1]], axis=1)[0:1, :]
    coeff = 0.7978845608028654
    dn[:, : 2 * shard] = dot_nt(n[...], cols[...])
    for d in range(spots):
        part = slice(d * rows, (d + 1) * rows)
        value = dn[part, : 2 * shard]
        square = value * value
        tangent = jnp.tanh(coeff * (value + 0.044715 * value * square))
        half = 0.5 * (1.0 + tangent)
        slope = half + 0.5 * value * (1.0 - tangent * tangent) * (
            coeff * (1.0 + 3.0 * 0.044715 * square)
        )
        g[part, :] = (weight * slope).astype(BF16)
        score = value * half * weight
        slots = rows // REGIONS
        folded = score[0:slots]
        for p in range(1, REGIONS):
            folded = folded + score[p * slots : (p + 1) * slots]
        ssend[d] = jnp.broadcast_to(jnp.sum(folded, axis=1, keepdims=True), ssend.shape[1:])
    dn[...] = dot_nn(g[...], cols[...])
    slot = lax.rem(lax.broadcasted_iota(jnp.int32, (rows, 1), 0), rows // REGIONS) + ctx * (
        2 * SUB
    )
    present = jnp.where((slot == 0) | (slot >= SUB), 1.0, 0.0)
    row_scale = present * (-LOSS_WEIGHT / REGIONS / span)
    for d in range(spots):
        part = slice(d * rows, (d + 1) * rows)
        value = dn[part, :]
        normed = u[part, :]
        first = jnp.mean(value, axis=-1, keepdims=True)
        second = jnp.mean(value * normed, axis=-1, keepdims=True)
        du[part, :] = (
            (value - first - normed * second) * (uscale[part, 0:1] * row_scale)
        ).astype(BF16)
    back = dot_nt(du[...], proj[...])
    for d in range(spots):
        dsend[d] = back[d * rows : (d + 1) * rows].astype(BF16)

    move_dem, move_sco = [], []
    for d in order:
        copy = pltpu.make_async_remote_copy(
            src_ref=dsend.at[d],
            dst_ref=drecv.at[d],
            send_sem=dem_send.at[d],
            recv_sem=dem_recv.at[d],
            device_id=downs[d],
            device_id_type=MESH,
        )
        copy.start()
        move_dem.append(copy)
    for d in order:
        copy = pltpu.make_async_remote_copy(
            src_ref=ssend.at[d],
            dst_ref=srecv.at[d],
            send_sem=sco_send.at[d],
            recv_sem=sco_recv.at[d],
            device_id=downs[d],
            device_id_type=MESH,
        )
        copy.start()
        move_sco.append(copy)

    demb = back[0:rows]
    for copy in move_dem:
        copy.wait_recv()
    for d in range(1, spots):
        demb = demb + drecv[d].astype(F32)
    emb32[...] = demb

    for f in range(2):
        for j in range(SUB):
            part = slice(j * channels, (j + 1) * channels)
            spread = jnp.concatenate(
                [
                    jnp.broadcast_to(
                        emb32[p * 2 * SUB + f * SUB + j : p * 2 * SUB + f * SUB + j + 1, :],
                        (span, channels),
                    )
                    for p in range(REGIONS)
                ],
                axis=0,
            )
            da1[f * TPF : (f + 1) * TPF, part] = (
                spread * a1[f * TPF : (f + 1) * TPF, part]
            ).astype(BF16)
        dfeat = dot_nt(da1[f * TPF : (f + 1) * TPF, :], up[...])
        part = slice(f * channels, (f + 1) * channels)
        da0[:, part] = (dfeat * a0[:, part]).astype(BF16)
    hsend[...] = dot_nt(da0[...], conv[0 : 2 * patch, :]).astype(BF16)
    move_h = far(hsend, hrecv, 3, before)
    own = dot_nt(da0[...], conv[2 * patch :, :])

    total = ssend[0]
    for copy in move_sco:
        copy.wait_recv()
    for d in range(1, spots):
        total = total + srecv[d]
    slots = total.shape[0]
    index = lax.broadcasted_iota(jnp.int32, total.shape, 0)
    lane = lax.broadcasted_iota(jnp.int32, total.shape, 1)
    where = index + ctx * slots
    total = jnp.where((where == 0) | (where >= SUB), total / REGIONS, 0.0)
    reward_out[...] = jnp.sum(jnp.where(index == lane, total, 0.0), axis=0, keepdims=True)

    move_h.wait_recv()
    live_after = jnp.where(ctx < steps - 1, 1.0, 0.0)
    grad = (-sigma) * (own + hrecv[...].astype(F32) * live_after)
    lean = (rstd[...] * grad).astype(BF16).astype(F32)
    one = lean * head_sums
    two = lean * vel0[...]
    place = lax.broadcasted_iota(jnp.int32, (TPF, 2 * patch), 1)
    for f in range(2):
        mine = left if f == 0 else jnp.logical_not(left)
        spot = 0 if f == 0 else patch
        mean_one = jnp.sum(jnp.where(mine, one, 0.0), axis=1, keepdims=True) / full
        mean_two = jnp.sum(jnp.where(mine, two, 0.0), axis=1, keepdims=True) / full
        slope = rstd[:, spot : spot + 1] * mean_two
        offset = slope * mean[:, spot : spot + 1] - mean_one
        high = offset.astype(BF16).astype(F32)
        middle = (offset - high).astype(BF16).astype(F32)
        low = offset - high - middle
        tail = jnp.where(
            place == patch,
            high,
            jnp.where(place == patch + 1, middle, jnp.where(place == patch + 2, low, 0.0)),
        )
        body = lean if f == 0 else pltpu.roll(lean, patch, 1)
        lhs_out[f * TPF : (f + 1) * TPF, :] = jnp.where(left, body, tail).astype(BF16)
        coef_out[f * TPF : (f + 1) * TPF, :] = jnp.broadcast_to(slope, (TPF, 2 * patch))

    for copy in [move_x, move_cols, move_vec, move_h] + move_emb + move_dem + move_sco:
        copy.wait_send()


def tail_kernel(hidden, modulation, head_weight, lhs, coef, rewards, grad, reward_out):
    patch, width = head_weight.shape
    scaled = (head_weight[...].astype(F32) * (1.0 + modulation[1:2, :])).astype(BF16)
    weight = jnp.concatenate([scaled, jnp.ones((patch, width), BF16)], axis=0)
    lanes = coef.shape[1]
    block = 16
    product = dot_nn(lhs[...], weight)
    for r in range(0, hidden.shape[0], block):
        slope = coef[r : r + block, :]
        for c in range(0, width, lanes):
            value = hidden[r : r + block, c : c + lanes].astype(F32)
            grad[r : r + block, c : c + lanes] = (
                product[r : r + block, c : c + lanes] - value * slope
            ).astype(BF16)
    reward_out[...] = rewards[:, : reward_out.shape[1]]


def per_device(
    hidden,
    modulation,
    head_weight,
    noisy,
    timestep,
    conv_weight,
    up_weight,
    patch_proj,
    fc1,
    reward_vec,
):
    states = hidden[0]
    tokens, full = states.shape
    patch = head_weight.shape[0]
    channels = up_weight.shape[1]
    features_r, shard = fc1.shape
    spots = lax.axis_size("fsdp") // 2
    rows = 2 * SUB * REGIONS
    slots = 2 * SUB
    lanes = 2 * patch
    width = 512
    chunks = full // width
    wide = max(features_r, 2 * shard)

    def vmem(shape, dtype):
        return pltpu.VMEM(shape, dtype)

    scratch = [
        vmem((chunks, tokens, width), BF16),
        vmem((2, full), F32),
        vmem((patch, full), BF16),
        vmem((patch, tokens), BF16),
        vmem((4 * patch, 2 * channels), BF16),
        vmem((channels, SUB * channels), BF16),
        vmem((channels, features_r), BF16),
        vmem((2 * shard, features_r), BF16),
        vmem((2, 8, shard), F32),
        vmem((1, shard), BF16),
        vmem((tokens, lanes), F32),
        vmem((32, lanes), F32),
        vmem((tokens, lanes), F32),
        vmem((tokens, lanes), F32),
        vmem((TPF, lanes), F32),
        vmem((TPF, lanes), F32),
        vmem((TPF, lanes), F32),
        vmem((TPF, lanes), BF16),
        vmem((TPF, lanes), BF16),
        vmem((TPF, 2 * channels), F32),
        vmem((tokens, channels), BF16),
        vmem((tokens, SUB * channels), F32),
        vmem((rows, channels), F32),
        vmem((spots, rows, channels), BF16),
        vmem((spots * rows, features_r), F32),
        vmem((spots * rows, 128), F32),
        vmem((spots * rows, features_r), BF16),
        vmem((spots * rows, 2 * shard), BF16),
        vmem((spots * rows, wide), F32),
        vmem((spots * rows, features_r), BF16),
        vmem((spots, rows, channels), BF16),
        vmem((spots, rows, channels), BF16),
        vmem((spots, slots, 128), F32),
        vmem((spots, slots, 128), F32),
        vmem((tokens, SUB * channels), BF16),
        vmem((TPF, 2 * channels), BF16),
        vmem((TPF, lanes), BF16),
        vmem((TPF, lanes), BF16),
        pltpu.SemaphoreType.DMA((chunks,)),
        pltpu.SemaphoreType.DMA((16,)),
        pltpu.SemaphoreType.DMA((4,)),
        pltpu.SemaphoreType.DMA((4,)),
        pltpu.SemaphoreType.DMA((spots,)),
        pltpu.SemaphoreType.DMA((spots,)),
        pltpu.SemaphoreType.DMA((spots,)),
        pltpu.SemaphoreType.DMA((spots,)),
        pltpu.SemaphoreType.DMA((spots,)),
        pltpu.SemaphoreType.DMA((spots,)),
    ]
    anywhere = pl.BlockSpec(memory_space=pl.ANY)
    local = pl.BlockSpec(memory_space=pltpu.VMEM)
    lhs, coef, rewards = pl.pallas_call(
        main_kernel,
        out_shape=(
            jax.ShapeDtypeStruct((tokens, lanes), BF16),
            jax.ShapeDtypeStruct((tokens, lanes), F32),
            jax.ShapeDtypeStruct((1, 128), F32),
        ),
        in_specs=[pl.BlockSpec(memory_space=pltpu.SMEM)] + [anywhere] * 9,
        out_specs=(local, local, local),
        scratch_shapes=scratch,
        compiler_params=pltpu.CompilerParams(
            collective_id=0, has_side_effects=True, vmem_limit_bytes=36 * 1024 * 1024
        ),
        name="reward_step",
    )(
        timestep,
        states,
        modulation,
        head_weight,
        noisy[0].T,
        conv_weight,
        up_weight,
        patch_proj,
        fc1.T,
        reward_vec,
    )
    piece = 512
    grad, reward = pl.pallas_call(
        tail_kernel,
        grid=(full // piece,),
        out_shape=(
            jax.ShapeDtypeStruct((tokens, full), BF16),
            jax.ShapeDtypeStruct((1, slots), F32),
        ),
        in_specs=[
            pl.BlockSpec((tokens, piece), lambda i: (0, i)),
            pl.BlockSpec((2, piece), lambda i: (0, i)),
            pl.BlockSpec((patch, piece), lambda i: (0, i)),
            pl.BlockSpec((tokens, lanes), lambda i: (0, 0)),
            pl.BlockSpec((tokens, lanes), lambda i: (0, 0)),
            pl.BlockSpec((1, 128), lambda i: (0, 0)),
        ],
        out_specs=(
            pl.BlockSpec((tokens, piece), lambda i: (0, i)),
            pl.BlockSpec((1, slots), lambda i: (0, 0)),
        ),
        compiler_params=pltpu.CompilerParams(vmem_limit_bytes=16 * 1024 * 1024),
        name="hidden_gradient",
    )(states, modulation, head_weight, lhs, coef, rewards)
    return (grad[None], reward)


def solution(mesh):
    return jax.shard_map(
        per_device,
        mesh=mesh,
        in_specs=(
            P("fsdp", "ctx", None),
            P(),
            P(),
            P("fsdp", "ctx", None),
            P(),
            P(),
            P(),
            P(),
            P(None, "fsdp"),
            P(None, "fsdp"),
        ),
        out_specs=(P("fsdp", "ctx", None), P("fsdp", "ctx")),
        check_vma=False,
    )
```

```python
import jax
import jax.numpy as jnp
from jax import lax
from jax.experimental import pallas as pl
from jax.experimental.pallas import tpu as pltpu
from jax.sharding import PartitionSpec as P

TPF = 224
REGIONS = 4
SUB = 4
LOSS_WEIGHT = 65536.0
EPSILON = 1e-06
F32 = jnp.float32
BF16 = jnp.bfloat16
MESH = pl.DeviceIdType.MESH


def dot_nn(a, b):
    return lax.dot_general(a, b, (((1,), (0,)), ((), ())), preferred_element_type=F32)


def dot_nt(a, b):
    return lax.dot_general(a, b, (((1,), (1,)), ((), ())), preferred_element_type=F32)


def sigmoid(value):
    return 0.5 + 0.5 * jnp.tanh(0.5 * value)


def silu(value):
    half = 0.5 * value
    return half + half * jnp.tanh(half)


def silu_slope(value):
    half = 0.5 * value
    tangent = jnp.tanh(half)
    return (0.5 + 0.5 * tangent) * (1.0 + half * (1.0 - tangent))


def lane_sums(value, pattern):
    high = value.astype(BF16)
    low = (value - high.astype(F32)).astype(BF16)
    return dot_nn(high, pattern) + dot_nn(low, pattern)


def main_kernel(
    timestep_in,
    hidden,
    modulation,
    head_weight,
    noisy_t,
    conv_weight,
    up_weight,
    patch_proj,
    fc1_t,
    reward_vec,
    hid,
    wide,
    lhs_out,
    coef_out,
    reward_out,
    timestep,
    mod,
    head,
    noisy,
    conv,
    up,
    proj,
    cols,
    mixed,
    vec,
    vec_in,
    acc,
    ssq,
    pilot,
    sums_part,
    shift_part,
    latents,
    vel0,
    rstd,
    mean,
    xown,
    xhalo,
    a0,
    feat,
    a1,
    emb32,
    emb,
    eall,
    terms,
    factors,
    g,
    dsend,
    drecv,
    ssend,
    srecv,
    da1,
    da0,
    hsend,
    hrecv,
    hid_sem,
    in_sem,
    far_send,
    far_recv,
    emb_send,
    emb_recv,
    dem_send,
    dem_recv,
    sco_send,
    sco_recv,
):
    chunks, tokens, width = hid.shape
    full = chunks * width
    patch = head.shape[0]
    lanes = 2 * patch
    channels = up.shape[0]
    features_r = proj.shape[1]
    shard = fc1_t.shape[0]
    span = TPF // REGIONS
    rows = eall.shape[1]
    slices = eall.shape[0]
    spots = lax.axis_size("fsdp") // 2
    slots = 2 * SUB
    block = 16
    padded = cols.shape[0]

    ctx, fsdp = lax.axis_index("ctx"), lax.axis_index("fsdp")
    steps = lax.axis_size("ctx")
    z, core = fsdp // 2, fsdp % 2
    after = (lax.rem(ctx + 1, steps), fsdp)
    before = (lax.rem(ctx + steps - 1, steps), fsdp)
    twin = (ctx, z * 2 + 1 - core)
    side = 1 - 2 * lax.rem(z, 2)

    def other_core(offset):
        return (ctx, lax.rem(z + offset * side + spots, spots) * 2 + 1 - core)

    ups = [other_core(offset) for offset in (0, -1, 2, -3)]
    downs = [other_core(offset) for offset in (0, -1, -2, -3)]
    pair = (ctx, (z + side) * 2 + core)
    reach = [other_core(offset) for offset in (0, -1, -2, -3, 2)] + [pair]
    has_before, has_after = ctx > 0, ctx < steps - 1

    loads = []

    def load(source, target):
        copy = pltpu.make_async_copy(source, target, in_sem.at[len(loads)])
        copy.start()
        loads.append(copy)
        return copy

    load_proj = load(patch_proj, proj.at[pl.ds(0, channels)])
    load_cols = load(fc1_t, cols.at[pl.ds(0, shard)])
    load_mod = load(modulation, mod)
    load_head = load(head_weight, head)
    hid_loads = []
    for k in range(chunks):
        copy = pltpu.make_async_copy(
            hidden.at[:, pl.ds(k * width, width)], hid.at[k], hid_sem.at[k]
        )
        copy.start()
        hid_loads.append(copy)

    barrier = pltpu.get_barrier_semaphore()
    for peer in reach:
        pl.semaphore_signal(barrier, inc=1, device_id=peer, device_id_type=MESH)

    @pl.when(has_after)
    def _():
        pl.semaphore_signal(barrier, inc=1, device_id=after, device_id_type=MESH)

    @pl.when(has_before)
    def _():
        pl.semaphore_signal(barrier, inc=1, device_id=before, device_id_type=MESH)

    load_noisy = load(noisy_t, noisy)
    load_step = load(timestep_in, timestep)
    load_vec = load(reward_vec, vec_in)
    load_conv = []
    for frame in range(2):
        for lag in range(3):
            spot = frame + 2 - lag
            load_conv.append(
                load(
                    conv_weight.at[lag],
                    conv.at[pl.ds(spot * patch, patch), pl.ds(frame * channels, channels)],
                )
            )
    load_up = [
        load(up_weight.at[j], up.at[:, pl.ds(j * channels, channels)]) for j in range(SUB)
    ]

    proj[channels:, :] = jnp.ones((proj.shape[0] - channels, features_r), BF16)
    cols[shard:, :] = jnp.ones((padded - shard, features_r), BF16)
    vec[0] = jnp.zeros(vec.shape[1:], F32)

    @pl.when(jnp.logical_not(has_before))
    def _():
        xhalo[...] = jnp.zeros_like(xhalo)

    @pl.when(jnp.logical_not(has_after))
    def _():
        hrecv[...] = jnp.zeros_like(hrecv)

    empty = jnp.zeros((patch, channels), BF16)
    conv[0:patch, channels:] = empty
    conv[3 * patch :, :channels] = empty
    for k in range(chunks):
        wide[k, patch:, :] = jnp.ones((patch, width), BF16)

    def lane_at(shape):
        return lax.broadcasted_iota(jnp.int32, shape, 1)

    left = lane_at((TPF, lanes)) < patch
    row_id = lax.broadcasted_iota(jnp.int32, (lanes, lanes), 0)
    col_id = lane_at((lanes, lanes))
    to_left = jnp.where(col_id < patch, 1.0, 0.0).astype(BF16)
    to_right = jnp.where(col_id < patch, 0.0, 1.0).astype(BF16)
    each_half = jnp.where((row_id < patch) == (col_id < patch), 1.0, 0.0).astype(BF16)

    def prepare():
        for r in range(0, patch, block):
            part = slice(r, r + block)
            cs = jnp.zeros((block, lanes), F32)
            bw = jnp.zeros((block, lanes), F32)
            for c in range(0, full, lanes):
                columns = slice(c, c + lanes)
                plain = head[part, columns].astype(F32)
                scaled = (plain * (1.0 + mod[1:2, columns])).astype(BF16)
                wide[c // width, part, c % width : c % width + lanes] = scaled
                cs = cs + scaled.astype(F32)
                bw = bw + plain * mod[0:1, columns]
            sums_part[part, :], shift_part[part, :] = cs, bw

    def features(group):
        first = group[0] == 0
        product = dot_nt(hid[group[0]], wide[group[0]])
        for k in group[1:]:
            product = product + dot_nt(hid[k], wide[k])
        acc[...] = product if first else acc[...] + product
        for r in range(0, tokens, block):
            part = slice(r, r + block)
            centre = pilot[part, :]
            total = jnp.zeros((block, lanes), F32) if first else ssq[part, :]
            for k in group:
                for c in range(0, width, lanes):
                    value = hid[k, part, c : c + lanes].astype(F32) - centre
                    total = total + value * value
            ssq[part, :] = total

    def phase_mixed():
        product = dot_nt(proj[...], cols[...])
        centre = product[0:channels, shard : shard + 1] / features_r
        mixed[:, 0:padded] = jnp.where(
            lane_at((channels, padded)) < shard,
            product[0:channels, :] - centre * product[channels : channels + 1, :],
            0.0,
        ).astype(BF16)

    def phase_gram():
        gram = dot_nt(proj[...], proj[0:channels, :]) / features_r
        centre = jnp.sum(proj[0:channels, :].astype(F32), axis=1, keepdims=True) / features_r
        gram = gram[0:channels, :] - centre * gram[channels : channels + 1, :]
        high = gram.astype(BF16)
        mixed[:, 4 * padded : 4 * padded + channels] = high
        mixed[:, 4 * padded + channels :] = (gram - high.astype(F32)).astype(BF16)

    def column_sums(part):
        high = part.astype(BF16)
        rest = part - high.astype(F32)
        middle = rest.astype(BF16)
        low = (rest - middle.astype(F32)).astype(BF16)
        ones = jnp.ones((8, lanes), BF16)
        total = dot_nt(ones, jnp.concatenate([high, high], axis=0))
        total = total + dot_nt(ones, jnp.concatenate([middle, middle], axis=0))
        return (total + dot_nt(ones, jnp.concatenate([low, low], axis=0)))[0:1, :]

    load_proj.wait()
    load_cols.wait()
    phase_mixed()
    load_mod.wait()
    load_head.wait()
    prepare()
    head_sums = column_sums(sums_part[...])
    head_shift = column_sums(shift_part[...])
    hid_loads[0].wait()
    pilot[...] = jnp.broadcast_to(hid[0, :, 0:1].astype(F32), pilot.shape)
    groups = [[0]] + [list(range(k, min(k + 2, chunks))) for k in range(1, chunks, 2)]
    for group in groups:
        for k in group:
            if k > 0:
                hid_loads[k].wait()
        if group is groups[-1]:
            load_noisy.wait()
            twice = jnp.concatenate([noisy[...], noisy[...]], axis=0)
            token = lax.broadcasted_iota(jnp.int32, (TPF, 2 * TPF), 0)
            place = lane_at((TPF, 2 * TPF))
            latents[...] = jnp.where(
                left,
                dot_nt(jnp.where(token == place, 1.0, 0.0).astype(BF16), twice),
                dot_nt(jnp.where(token + TPF == place, 1.0, 0.0).astype(BF16), twice),
            )
        features(group)
    load_step.wait()
    step_frac = timestep[0:1, 0:lanes].astype(F32) / 1000.0
    sigma = 5.0 * step_frac / (1.0 + 4.0 * step_frac)

    reached = len(reach) + jnp.where(has_before, 1, 0) + jnp.where(has_after, 1, 0)
    pl.semaphore_wait(barrier, reached)

    def far(source, target, index, device):
        return pltpu.make_async_remote_copy(
            src_ref=source,
            dst_ref=target,
            send_sem=far_send.at[index],
            recv_sem=far_recv.at[index],
            device_id=device,
            device_id_type=MESH,
        )

    def share(index, source, target, device):
        moves = [
            far(
                mixed.at[:, pl.ds(source * padded, padded)],
                mixed.at[:, pl.ds(target * padded, padded)],
                index,
                device,
            ),
            far(vec.at[source], vec.at[target], index + 1, device),
        ]
        for move in moves:
            move.start()
        return moves

    load_vec.wait()
    vec[0, :, 0:shard] = jnp.broadcast_to(vec_in[...].astype(F32), (vec.shape[1], shard))
    share_pair = share(2, 0, 1, pair)
    share_twin = share(4, 0, 2, twin)

    def phase_latents():
        one, two = acc[0:TPF, :], acc[TPF:, :]
        average = jnp.where(left, pltpu.roll(one, patch, 1), two) / full
        product = jnp.where(left, one, pltpu.roll(two, patch, 1))
        off = average - jnp.where(left, pilot[0:TPF, :], pilot[TPF:, :])
        square = lane_sums(ssq[0:TPF, :], to_left) + lane_sums(ssq[TPF:, :], to_right)
        var = jnp.maximum(square / full - off * off, 0.0)
        scale = lax.rsqrt(var + EPSILON)
        mean[...] = average
        rstd[...] = scale
        velocity = scale * (product - average * head_sums)
        vel0[...] = velocity
        xown[...] = (latents[...] - sigma * (velocity + head_shift)).astype(BF16)

    phase_latents()

    move_x = far(xown, xhalo, 0, after)

    @pl.when(has_after)
    def _():
        move_x.start()

    phase_gram()
    for copy in load_conv + load_up:
        copy.wait()
    a0[...] = dot_nn(xown[...], conv[2 * patch :, :])

    @pl.when(has_before)
    def _():
        move_x.wait_recv()

    def phase_feat():
        a0[...] += dot_nn(xhalo[...], conv[0 : 2 * patch, :])
        for f in range(2):
            for r in range(0, TPF, block):
                value = a0[r : r + block, f * channels : (f + 1) * channels]
                feat[f * TPF + r : f * TPF + r + block, :] = silu(value).astype(BF16)

    phase_feat()

    def phase_upsample():
        for j in range(SUB):
            part = slice(j * channels, (j + 1) * channels)
            a1[:, part] = dot_nn(feat[...], up[:, part])
            for f in range(2):
                for p in range(REGIONS):
                    begin = f * TPF + p * span
                    pooled = jnp.sum(
                        silu(a1[begin : begin + span, part]), axis=0, keepdims=True
                    )
                    row = p * slots + f * SUB + j
                    emb32[row : row + 1, :] = pooled / span

    phase_upsample()
    emb[...] = emb32[...].astype(BF16)

    order = list(range(slices - 1, -1, -1))
    near, distant = [0, 1], [2, 3]
    line = near + distant

    move_emb = {}
    for d in order:
        move_emb[d] = pltpu.make_async_remote_copy(
            src_ref=emb,
            dst_ref=eall.at[d],
            send_sem=emb_send.at[d],
            recv_sem=emb_recv.at[d],
            device_id=ups[d],
            device_id_type=MESH,
        )
        move_emb[d].start()

    for move in share_pair:
        move.wait_recv()
    share_on = share(6, 1, 3, twin)

    def phase_slopes():
        for f in range(2):
            for r in range(0, TPF, block):
                for j in range(SUB):
                    part = slice(j * channels, (j + 1) * channels)
                    where = slice(f * TPF + r, f * TPF + r + block)
                    a1[where, part] = silu_slope(a1[where, part])
                part = slice(f * channels, (f + 1) * channels)
                a0[r : r + block, part] = silu_slope(a0[r : r + block, part])

    phase_slopes()
    for move in share_twin + share_on:
        move.wait_recv()
    weight = jnp.concatenate([vec[q] for q in range(4)], axis=1)[0:1, :]
    slot = lax.rem(lax.broadcasted_iota(jnp.int32, (rows, 1), 0), slots) + ctx * slots
    present = jnp.where((slot == 0) | (slot >= SUB), 1.0, 0.0)
    row_scale = present * (-LOSS_WEIGHT / REGIONS / span)

    def row_of(d):
        return line.index(d) * rows

    def all_rows(group):
        return slice(row_of(group[0]), row_of(group[-1]) + rows)

    def reward(group):
        part = all_rows(group)
        both = 4 * padded
        terms[part, :] = dot_nn(
            jnp.concatenate([eall[d] for d in group], axis=0), mixed[...]
        )
        coeff = 0.7978845608028654
        for d in group:
            total = None
            for r in range(0, rows, block):
                where = slice(row_of(d) + r, row_of(d) + r + block)
                pulled = terms[where, both : both + channels] + terms[where, both + channels :]
                own_emb = eall[d, r : r + block, :].astype(F32)
                var = jnp.sum(pulled * own_emb, axis=1, keepdims=True)
                scale = lax.rsqrt(jnp.maximum(var, 0.0) + EPSILON)
                value = terms[where, :both] * scale
                square = value * value
                tangent = jnp.tanh(value * (coeff + (coeff * 0.044715) * square))
                half = 0.5 * (1.0 + tangent)
                slope = half + 0.5 * value * (1.0 - tangent * tangent) * (
                    coeff + (coeff * 3.0 * 0.044715) * square
                )
                slope = (weight * slope).astype(BF16)
                g[where, :] = slope
                along = jnp.sum(slope.astype(F32) * value, axis=1, keepdims=True)
                factor = scale * row_scale[r : r + block]
                factors[where, :] = jnp.broadcast_to(factor, (block, 128))
                terms[where, both : both + channels] = pulled * (factor * scale * along)
                points = value * half * weight
                for q in range(0, block, slots):
                    for c in range(0, both, 128):
                        piece = points[q : q + slots, c : c + 128]
                        total = piece if total is None else total + piece
            ssend[d] = total

    def gradient(group):
        part = all_rows(group)
        both = 4 * padded
        back = dot_nt(g[part, :], mixed[:, 0:both])
        for d in group:
            where = slice(row_of(d), row_of(d) + rows)
            begin = row_of(d) - part.start
            dsend[d] = (
                back[begin : begin + rows] * factors[where, 0:1]
                - terms[where, both : both + channels]
            ).astype(BF16)

    move_dem, move_sco = {}, {}

    def send_back(group):
        for d in group:
            move_dem[d] = pltpu.make_async_remote_copy(
                src_ref=dsend.at[d],
                dst_ref=drecv.at[d],
                send_sem=dem_send.at[d],
                recv_sem=dem_recv.at[d],
                device_id=downs[d],
                device_id_type=MESH,
            )
            move_dem[d].start()

    for d in near:
        move_emb[d].wait_recv()

    def phase_near():
        reward(near)

    phase_near()
    for d in distant:
        move_emb[d].wait_recv()

    def phase_distant():
        reward(distant)
        gradient(distant)

    phase_distant()
    send_back(distant)

    def phase_nearback():
        gradient(near)

    phase_nearback()
    send_back(reversed(near))
    for d in order:
        move_sco[d] = pltpu.make_async_remote_copy(
            src_ref=ssend.at[d],
            dst_ref=srecv.at[d],
            send_sem=sco_send.at[d],
            recv_sem=sco_recv.at[d],
            device_id=downs[d],
            device_id_type=MESH,
        )
        move_sco[d].start()

    for d in order:
        move_dem[d].wait_recv()
    demb = drecv[0].astype(F32)
    for d in range(1, slices):
        demb = demb + drecv[d].astype(F32)
    emb32[...] = demb

    def phase_da0():
        for f in range(2):
            for j in range(SUB):
                part = slice(j * channels, (j + 1) * channels)
                spread = jnp.concatenate(
                    [
                        jnp.broadcast_to(
                            emb32[p * slots + f * SUB + j : p * slots + f * SUB + j + 1, :],
                            (span, channels),
                        )
                        for p in range(REGIONS)
                    ],
                    axis=0,
                )
                da1[f * TPF : (f + 1) * TPF, part] = (
                    spread * a1[f * TPF : (f + 1) * TPF, part]
                ).astype(BF16)
            dfeat = dot_nt(da1[f * TPF : (f + 1) * TPF, :], up[...])
            part = slice(f * channels, (f + 1) * channels)
            da0[:, part] = (dfeat * a0[:, part]).astype(BF16)

    phase_da0()

    def phase_hsend():
        hsend[...] = dot_nt(da0[...], conv[0 : 2 * patch, :]).astype(BF16)

    phase_hsend()
    move_h = far(hsend, hrecv, 1, before)

    @pl.when(has_before)
    def _():
        move_h.start()

    own = dot_nt(da0[...], conv[2 * patch :, :])

    for d in order:
        move_sco[d].wait_recv()
    total = srecv[0]
    for d in range(1, slices):
        total = total + srecv[d]
    total = jnp.sum(total, axis=1, keepdims=True) / REGIONS
    index = lax.broadcasted_iota(jnp.int32, (slots, 128), 0)
    where = index + ctx * slots
    keep = ((where == 0) | (where >= SUB)) & (index == lane_at((slots, 128)))
    reward_out[...] = jnp.sum(jnp.where(keep, total, 0.0), axis=0, keepdims=True)

    @pl.when(has_after)
    def _():
        move_h.wait_recv()

    def phase_final():
        grad = (-sigma) * (own + hrecv[...].astype(F32))
        lean = (rstd[...] * grad).astype(BF16).astype(F32)
        one = lane_sums(lean * head_sums, each_half) / full
        two = lane_sums(lean * vel0[...], each_half) / full
        slope = rstd[...] * two
        offset = slope * mean[...] - one
        high = offset.astype(BF16).astype(F32)
        middle = (offset - high).astype(BF16).astype(F32)
        low = offset - high - middle
        nth = lax.rem(lane_at((TPF, lanes)), patch)
        tail = jnp.where(nth == 0, high, jnp.where(nth == 1, middle, low))
        tail = jnp.where(nth < 3, tail, 0.0)
        other = pltpu.roll(slope, patch, 1)
        lhs_out[0:TPF, :] = jnp.where(left, lean, pltpu.roll(tail, patch, 1)).astype(BF16)
        lhs_out[TPF:, :] = jnp.where(left, pltpu.roll(lean, patch, 1), tail).astype(BF16)
        coef_out[0:TPF, :] = jnp.where(left, slope, other)
        coef_out[TPF:, :] = jnp.where(left, other, slope)

    phase_final()

    @pl.when(has_after)
    def _():
        move_x.wait_send()

    @pl.when(has_before)
    def _():
        move_h.wait_send()

    for move in share_pair + share_twin + share_on:
        move.wait_send()
    for d in order:
        move_emb[d].wait_send()
        move_dem[d].wait_send()
        move_sco[d].wait_send()


def tail_kernel(hid, wide, lhs, coef, rewards, grad, reward_out, held, sem):
    chunks, tokens, width = hid.shape
    lanes = coef.shape[1]
    piece = width // 2
    block = 16
    reward_out[...] = rewards[:, : reward_out.shape[1]]
    copies = []
    for k in range(chunks):
        for begin in range(0, width, piece):
            product = dot_nn(lhs[...], wide[k, :, begin : begin + piece])
            first = k * width + begin
            for r in range(0, tokens, block):
                part = slice(r, r + block)
                slope = coef[part, :]
                for c in range(0, piece, lanes):
                    value = hid[k, part, begin + c : begin + c + lanes].astype(F32)
                    held[part, first + c : first + c + lanes] = (
                        product[part, c : c + lanes] - value * slope
                    ).astype(BF16)
            columns = pl.ds(first, piece)
            copy = pltpu.make_async_copy(
                held.at[:, columns], grad.at[:, columns], sem.at[len(copies)]
            )
            copy.start()
            copies.append(copy)
    for copy in copies:
        copy.wait()


def per_device(
    hidden,
    modulation,
    head_weight,
    noisy,
    timestep,
    conv_weight,
    up_weight,
    patch_proj,
    fc1,
    reward_vec,
):
    states = hidden[0]
    tokens, full = states.shape
    patch = head_weight.shape[0]
    channels = up_weight.shape[1]
    features_r, shard = fc1.shape
    slices = 4
    rows = 2 * SUB * REGIONS
    slots = 2 * SUB
    lanes = 2 * patch
    width = 1024
    chunks = full // width
    padded = (shard // 128 + 1) * 128
    vmem = pltpu.VMEM

    scratch = [
        vmem((8, 128), jnp.int32),
        vmem((2, full), F32),
        vmem((patch, full), BF16),
        vmem((patch, tokens), BF16),
        vmem((4 * patch, 2 * channels), BF16),
        vmem((channels, SUB * channels), BF16),
        vmem((channels + 16, features_r), BF16),
        vmem((padded, features_r), BF16),
        vmem((channels, 4 * padded + 2 * channels), BF16),
        vmem((4, 8, padded), F32),
        vmem((1, shard), BF16),
        vmem((tokens, lanes), F32),
        vmem((tokens, lanes), F32),
        vmem((tokens, lanes), F32),
        vmem((patch, lanes), F32),
        vmem((patch, lanes), F32),
        vmem((TPF, lanes), F32),
        vmem((TPF, lanes), F32),
        vmem((TPF, lanes), F32),
        vmem((TPF, lanes), F32),
        vmem((TPF, lanes), BF16),
        vmem((TPF, lanes), BF16),
        vmem((TPF, 2 * channels), F32),
        vmem((tokens, channels), BF16),
        vmem((tokens, SUB * channels), F32),
        vmem((rows, channels), F32),
        vmem((rows, channels), BF16),
        vmem((slices, rows, channels), BF16),
        vmem((slices * rows, 4 * padded + 2 * channels), F32),
        vmem((slices * rows, 128), F32),
        vmem((slices * rows, 4 * padded), BF16),
        vmem((slices, rows, channels), BF16),
        vmem((slices, rows, channels), BF16),
        vmem((slices, slots, 128), F32),
        vmem((slices, slots, 128), F32),
        vmem((tokens, SUB * channels), BF16),
        vmem((TPF, 2 * channels), BF16),
        vmem((TPF, lanes), BF16),
        vmem((TPF, lanes), BF16),
        pltpu.SemaphoreType.DMA((chunks,)),
        pltpu.SemaphoreType.DMA((20,)),
        pltpu.SemaphoreType.DMA((8,)),
        pltpu.SemaphoreType.DMA((8,)),
        pltpu.SemaphoreType.DMA((slices,)),
        pltpu.SemaphoreType.DMA((slices,)),
        pltpu.SemaphoreType.DMA((slices,)),
        pltpu.SemaphoreType.DMA((slices,)),
        pltpu.SemaphoreType.DMA((slices,)),
        pltpu.SemaphoreType.DMA((slices,)),
    ]
    in_hbm = pl.BlockSpec(memory_space=pltpu.HBM)
    local = pl.BlockSpec(memory_space=pltpu.VMEM)
    hid, wide, lhs, coef, rewards = pl.pallas_call(
        main_kernel,
        out_shape=(
            vmem((chunks, tokens, width), BF16),
            vmem((chunks, lanes, width), BF16),
            vmem((tokens, lanes), BF16),
            vmem((tokens, lanes), F32),
            vmem((1, 128), F32),
        ),
        in_specs=[in_hbm] * 10,
        out_specs=(local,) * 5,
        scratch_shapes=scratch,
        compiler_params=pltpu.CompilerParams(
            collective_id=0, has_side_effects=True, vmem_limit_bytes=36 * 1024 * 1024
        ),
        name="reward_step",
    )(
        *(
            pltpu.with_memory_space_constraint(value, pltpu.HBM)
            for value in (
                jnp.broadcast_to(timestep, (8, 128)),
                states,
                modulation,
                head_weight,
                noisy[0].T,
                conv_weight,
                up_weight,
                patch_proj,
                fc1.T,
                reward_vec,
            )
        ),
    )
    grad, reward = pl.pallas_call(
        tail_kernel,
        out_shape=(
            jax.ShapeDtypeStruct((tokens, full), BF16),
            jax.ShapeDtypeStruct((1, slots), F32),
        ),
        in_specs=[local] * 5,
        out_specs=(in_hbm, local),
        scratch_shapes=[vmem((tokens, full), BF16), pltpu.SemaphoreType.DMA((2 * chunks,))],
        compiler_params=pltpu.CompilerParams(vmem_limit_bytes=20 * 1024 * 1024),
        name="hidden_gradient",
    )(hid, wide, lhs, coef, rewards)
    return (grad[None], reward)


def solution(mesh):
    return jax.shard_map(
        per_device,
        mesh=mesh,
        in_specs=(
            P("fsdp", "ctx", None),
            P(),
            P(),
            P("fsdp", "ctx", None),
            P(),
            P(),
            P(),
            P(),
            P(None, "fsdp"),
            P(None, "fsdp"),
        ),
        out_specs=(P("fsdp", "ctx", None), P("fsdp", "ctx")),
        check_vma=False,
    )
```

```python
import jax
import jax.numpy as jnp
from jax import lax
from jax.experimental import pallas as pl
from jax.experimental.pallas import tpu as pltpu
from jax.sharding import PartitionSpec as P

TPF = 224
REGIONS = 4
SUB = 4
LOSS_WEIGHT = 65536.0
EPSILON = 1e-06
F32 = jnp.float32
BF16 = jnp.bfloat16
MESH = pl.DeviceIdType.MESH


def dot_nn(a, b):
    return lax.dot_general(a, b, (((1,), (0,)), ((), ())), preferred_element_type=F32)


def dot_nt(a, b):
    return lax.dot_general(a, b, (((1,), (1,)), ((), ())), preferred_element_type=F32)


def sigmoid(value):
    return 0.5 + 0.5 * jnp.tanh(0.5 * value)


def silu(value):
    half = 0.5 * value
    return half + half * jnp.tanh(half)


def silu_slope(value):
    half = 0.5 * value
    tangent = jnp.tanh(half)
    return (0.5 + 0.5 * tangent) * (1.0 + half * (1.0 - tangent))


def lane_sums(value, pattern):
    high = value.astype(BF16)
    low = (value - high.astype(F32)).astype(BF16)
    return dot_nn(high, pattern) + dot_nn(low, pattern)


def main_kernel(
    timestep,
    hidden,
    modulation,
    head_weight,
    noisy_t,
    conv_weight,
    up_weight,
    patch_proj,
    fc1_t,
    reward_vec,
    hid,
    wide,
    lhs_out,
    coef_out,
    reward_out,
    mod,
    head,
    noisy,
    conv,
    up,
    proj,
    cols,
    mixed,
    vec,
    vec_in,
    acc,
    ssq,
    pilot,
    sums_part,
    shift_part,
    latents,
    vel0,
    rstd,
    mean,
    xown,
    xhalo,
    a0,
    feat,
    a1,
    emb32,
    emb,
    eall,
    terms,
    factors,
    g,
    dsend,
    drecv,
    ssend,
    srecv,
    da1,
    da0,
    hsend,
    hrecv,
    hid_sem,
    in_sem,
    far_send,
    far_recv,
    emb_send,
    emb_recv,
    dem_send,
    dem_recv,
    sco_send,
    sco_recv,
):
    chunks, tokens, width = hid.shape
    full = chunks * width
    patch = head.shape[0]
    lanes = 2 * patch
    channels = up.shape[0]
    features_r = proj.shape[1]
    shard = fc1_t.shape[0]
    span = TPF // REGIONS
    rows = eall.shape[1]
    slices = eall.shape[0]
    spots = lax.axis_size("fsdp") // 2
    slots = 2 * SUB
    block = 16

    ctx, fsdp = lax.axis_index("ctx"), lax.axis_index("fsdp")
    steps = lax.axis_size("ctx")
    z, core = fsdp // 2, fsdp % 2
    after = (lax.rem(ctx + 1, steps), fsdp)
    before = (lax.rem(ctx + steps - 1, steps), fsdp)
    twin = (ctx, z * 2 + 1 - core)
    side = 1 - 2 * lax.rem(z, 2)

    def other_core(offset):
        return (ctx, lax.rem(z + offset * side + spots, spots) * 2 + 1 - core)

    ups = [other_core(offset) for offset in (0, -1, 2, -3)]
    downs = [other_core(offset) for offset in (0, -1, -2, -3)]
    pair = (ctx, (z + side) * 2 + core)
    reach = [other_core(offset) for offset in (0, -1, -2, -3, 2)] + [pair]
    has_before, has_after = ctx > 0, ctx < steps - 1

    loads = []

    def load(source, target):
        copy = pltpu.make_async_copy(source, target, in_sem.at[len(loads)])
        copy.start()
        loads.append(copy)
        return copy

    load_proj = load(patch_proj, proj.at[pl.ds(0, channels)])
    load_cols = load(fc1_t, cols.at[pl.ds(0, shard)])
    load_mod = load(modulation, mod)
    load_head = load(head_weight, head)
    hid_loads = []
    for k in range(chunks):
        copy = pltpu.make_async_copy(
            hidden.at[:, pl.ds(k * width, width)], hid.at[k], hid_sem.at[k]
        )
        copy.start()
        hid_loads.append(copy)

    barrier = pltpu.get_barrier_semaphore()
    for peer in reach:
        pl.semaphore_signal(barrier, inc=1, device_id=peer, device_id_type=MESH)

    @pl.when(has_after)
    def _():
        pl.semaphore_signal(barrier, inc=1, device_id=after, device_id_type=MESH)

    @pl.when(has_before)
    def _():
        pl.semaphore_signal(barrier, inc=1, device_id=before, device_id_type=MESH)

    load_noisy = load(noisy_t, noisy)
    load_vec = load(reward_vec, vec_in)
    load_conv = []
    for frame in range(2):
        for lag in range(3):
            spot = frame + 2 - lag
            load_conv.append(
                load(
                    conv_weight.at[lag],
                    conv.at[pl.ds(spot * patch, patch), pl.ds(frame * channels, channels)],
                )
            )
    load_up = [
        load(up_weight.at[j], up.at[:, pl.ds(j * channels, channels)]) for j in range(SUB)
    ]

    proj[channels:, :] = jnp.ones((proj.shape[0] - channels, features_r), BF16)
    cols[shard:, :] = jnp.ones((cols.shape[0] - shard, features_r), BF16)

    @pl.when(jnp.logical_not(has_before))
    def _():
        xhalo[...] = jnp.zeros_like(xhalo)

    @pl.when(jnp.logical_not(has_after))
    def _():
        hrecv[...] = jnp.zeros_like(hrecv)

    empty = jnp.zeros((patch, channels), BF16)
    conv[0:patch, channels:] = empty
    conv[3 * patch :, :channels] = empty
    for k in range(chunks):
        wide[k, patch:, :] = jnp.ones((patch, width), BF16)

    def lane_at(shape):
        return lax.broadcasted_iota(jnp.int32, shape, 1)

    left = lane_at((TPF, lanes)) < patch
    row_id = lax.broadcasted_iota(jnp.int32, (lanes, lanes), 0)
    col_id = lane_at((lanes, lanes))
    to_left = jnp.where(col_id < patch, 1.0, 0.0).astype(BF16)
    to_right = jnp.where(col_id < patch, 0.0, 1.0).astype(BF16)
    each_half = jnp.where((row_id < patch) == (col_id < patch), 1.0, 0.0).astype(BF16)

    def prepare():
        for r in range(0, patch, block):
            part = slice(r, r + block)
            cs = jnp.zeros((block, lanes), F32)
            bw = jnp.zeros((block, lanes), F32)
            for c in range(0, full, lanes):
                columns = slice(c, c + lanes)
                plain = head[part, columns].astype(F32)
                scaled = (plain * (1.0 + mod[1:2, columns])).astype(BF16)
                wide[c // width, part, c % width : c % width + lanes] = scaled
                cs = cs + scaled.astype(F32)
                bw = bw + plain * mod[0:1, columns]
            sums_part[part, :], shift_part[part, :] = cs, bw

    def features(group):
        first = group[0] == 0
        product = dot_nt(hid[group[0]], wide[group[0]])
        for k in group[1:]:
            product = product + dot_nt(hid[k], wide[k])
        acc[...] = product if first else acc[...] + product
        for r in range(0, tokens, block):
            part = slice(r, r + block)
            centre = pilot[part, :]
            total = jnp.zeros((block, lanes), F32) if first else ssq[part, :]
            for k in group:
                for c in range(0, width, lanes):
                    value = hid[k, part, c : c + lanes].astype(F32) - centre
                    total = total + value * value
            ssq[part, :] = total

    def phase_mixed():
        product = dot_nt(cols[...], proj[...])
        centre = product[shard : shard + 1, 0:channels] / features_r
        mixed[0:shard, :] = (
            product[0:shard, 0:channels] - product[0:shard, channels : channels + 1] * centre
        ).astype(BF16)

    def phase_gram():
        gram = dot_nt(proj[...], proj[0:channels, :]) / features_r
        centre = jnp.sum(proj[0:channels, :].astype(F32), axis=1, keepdims=True) / features_r
        gram = gram[0:channels, :] - centre * gram[channels : channels + 1, :]
        high = gram.astype(BF16)
        mixed[4 * shard : 4 * shard + channels, :] = high
        mixed[4 * shard + channels :, :] = (gram - high.astype(F32)).astype(BF16)

    def column_sums(part):
        high = part.astype(BF16)
        rest = part - high.astype(F32)
        middle = rest.astype(BF16)
        low = (rest - middle.astype(F32)).astype(BF16)
        ones = jnp.ones((8, lanes), BF16)
        total = dot_nt(ones, jnp.concatenate([high, high], axis=0))
        total = total + dot_nt(ones, jnp.concatenate([middle, middle], axis=0))
        return (total + dot_nt(ones, jnp.concatenate([low, low], axis=0)))[0:1, :]

    def far(source, target, index, device):
        return pltpu.make_async_remote_copy(
            src_ref=source,
            dst_ref=target,
            send_sem=far_send.at[index],
            recv_sem=far_recv.at[index],
            device_id=device,
            device_id_type=MESH,
        )

    def share(index, source, target, device):
        moves = [
            far(
                mixed.at[pl.ds(source * shard, shard)],
                mixed.at[pl.ds(target * shard, shard)],
                index,
                device,
            ),
            far(vec.at[source], vec.at[target], index + 1, device),
        ]
        for move in moves:
            move.start()
        return moves

    load_proj.wait()
    load_cols.wait()
    phase_mixed()
    load_vec.wait()
    vec[0] = jnp.broadcast_to(vec_in[...].astype(F32), vec.shape[1:])
    load_mod.wait()
    load_head.wait()
    prepare()
    head_sums = column_sums(sums_part[...])
    head_shift = column_sums(shift_part[...])
    hid_loads[0].wait()
    pilot[...] = jnp.broadcast_to(hid[0, :, 0:1].astype(F32), pilot.shape)
    groups = [[0]] + [list(range(k, min(k + 2, chunks))) for k in range(1, chunks, 2)]
    for group in groups:
        for k in group:
            if k > 0:
                hid_loads[k].wait()
        if group is groups[-1]:
            load_noisy.wait()
            twice = jnp.concatenate([noisy[...], noisy[...]], axis=0)
            token = lax.broadcasted_iota(jnp.int32, (TPF, 2 * TPF), 0)
            place = lane_at((TPF, 2 * TPF))
            latents[...] = jnp.where(
                left,
                dot_nt(jnp.where(token == place, 1.0, 0.0).astype(BF16), twice),
                dot_nt(jnp.where(token + TPF == place, 1.0, 0.0).astype(BF16), twice),
            )
        features(group)
        if group is groups[0]:
            reached = len(reach) + jnp.where(has_before, 1, 0) + jnp.where(has_after, 1, 0)
            pl.semaphore_wait(barrier, reached)
            share_pair = share(2, 0, 1, pair)
            share_twin = share(4, 0, 2, twin)
    step_frac = jnp.full((1, lanes), timestep[0].astype(F32)) / 1000.0
    sigma = 5.0 * step_frac / (1.0 + 4.0 * step_frac)

    def phase_latents():
        one, two = acc[0:TPF, :], acc[TPF:, :]
        average = jnp.where(left, pltpu.roll(one, patch, 1), two) / full
        product = jnp.where(left, one, pltpu.roll(two, patch, 1))
        off = average - jnp.where(left, pilot[0:TPF, :], pilot[TPF:, :])
        square = lane_sums(ssq[0:TPF, :], to_left) + lane_sums(ssq[TPF:, :], to_right)
        var = jnp.maximum(square / full - off * off, 0.0)
        scale = lax.rsqrt(var + EPSILON)
        mean[...] = average
        rstd[...] = scale
        velocity = scale * (product - average * head_sums)
        vel0[...] = velocity
        xown[...] = (latents[...] - sigma * (velocity + head_shift)).astype(BF16)

    phase_latents()

    move_x = far(xown, xhalo, 0, after)

    @pl.when(has_after)
    def _():
        move_x.start()

    phase_gram()
    for copy in load_conv + load_up:
        copy.wait()
    a0[...] = dot_nn(xown[...], conv[2 * patch :, :])

    @pl.when(has_before)
    def _():
        move_x.wait_recv()

    def phase_feat():
        a0[...] += dot_nn(xhalo[...], conv[0 : 2 * patch, :])
        for f in range(2):
            for r in range(0, TPF, block):
                value = a0[r : r + block, f * channels : (f + 1) * channels]
                feat[f * TPF + r : f * TPF + r + block, :] = silu(value).astype(BF16)

    phase_feat()

    def phase_upsample():
        for j in range(SUB):
            part = slice(j * channels, (j + 1) * channels)
            a1[:, part] = dot_nn(feat[...], up[:, part])
            for f in range(2):
                for p in range(REGIONS):
                    begin = f * TPF + p * span
                    pooled = jnp.sum(
                        silu(a1[begin : begin + span, part]), axis=0, keepdims=True
                    )
                    row = p * slots + f * SUB + j
                    emb32[row : row + 1, :] = pooled / span

    phase_upsample()
    emb[...] = emb32[...].astype(BF16)

    order = list(range(slices - 1, -1, -1))
    near, distant = [0, 1], [2, 3]
    line = near + distant

    move_emb = {}
    for d in order:
        move_emb[d] = pltpu.make_async_remote_copy(
            src_ref=emb,
            dst_ref=eall.at[d],
            send_sem=emb_send.at[d],
            recv_sem=emb_recv.at[d],
            device_id=ups[d],
            device_id_type=MESH,
        )
        move_emb[d].start()

    for move in share_pair:
        move.wait_recv()
    share_on = share(6, 1, 3, twin)

    def phase_slopes():
        for f in range(2):
            for r in range(0, TPF, block):
                for j in range(SUB):
                    part = slice(j * channels, (j + 1) * channels)
                    where = slice(f * TPF + r, f * TPF + r + block)
                    a1[where, part] = silu_slope(a1[where, part])
                part = slice(f * channels, (f + 1) * channels)
                a0[r : r + block, part] = silu_slope(a0[r : r + block, part])

    phase_slopes()
    for move in share_twin + share_on:
        move.wait_recv()
    weight = jnp.concatenate([vec[q] for q in range(4)], axis=1)[0:1, :]
    slot = lax.rem(lax.broadcasted_iota(jnp.int32, (rows, 1), 0), slots) + ctx * slots
    present = jnp.where((slot == 0) | (slot >= SUB), 1.0, 0.0)
    row_scale = present * (-LOSS_WEIGHT / REGIONS / span)

    def row_of(d):
        return line.index(d) * rows

    def all_rows(group):
        return slice(row_of(group[0]), row_of(group[-1]) + rows)

    def reward(group):
        part = all_rows(group)
        both = 4 * shard
        terms[part, :] = dot_nt(
            jnp.concatenate([eall[d] for d in group], axis=0), mixed[...]
        )
        coeff = 0.7978845608028654
        for d in group:
            total = None
            for r in range(0, rows, block):
                where = slice(row_of(d) + r, row_of(d) + r + block)
                pulled = terms[where, both : both + channels] + terms[where, both + channels :]
                own_emb = eall[d, r : r + block, :].astype(F32)
                var = jnp.sum(pulled * own_emb, axis=1, keepdims=True)
                scale = lax.rsqrt(jnp.maximum(var, 0.0) + EPSILON)
                value = terms[where, :both] * scale
                square = value * value
                tangent = jnp.tanh(value * (coeff + (coeff * 0.044715) * square))
                half = 0.5 * (1.0 + tangent)
                slope = half + 0.5 * value * (1.0 - tangent * tangent) * (
                    coeff + (coeff * 3.0 * 0.044715) * square
                )
                slope = (weight * slope).astype(BF16)
                g[where, :] = slope
                along = jnp.sum(slope.astype(F32) * value, axis=1, keepdims=True)
                factor = scale * row_scale[r : r + block]
                factors[where, :] = jnp.broadcast_to(factor, (block, 128))
                terms[where, both : both + channels] = pulled * (factor * scale * along)
                points = value * half * weight
                for q in range(0, block, slots):
                    for c in range(0, both, 128):
                        piece = points[q : q + slots, c : c + 128]
                        total = piece if total is None else total + piece
            ssend[d] = total

    def gradient(group):
        part = all_rows(group)
        both = 4 * shard
        back = dot_nn(g[part, :], mixed[0:both, :])
        for d in group:
            where = slice(row_of(d), row_of(d) + rows)
            begin = row_of(d) - part.start
            dsend[d] = (
                back[begin : begin + rows] * factors[where, 0:1]
                - terms[where, both : both + channels]
            ).astype(BF16)

    move_dem, move_sco = {}, {}

    def send_back(group):
        for d in group:
            move_dem[d] = pltpu.make_async_remote_copy(
                src_ref=dsend.at[d],
                dst_ref=drecv.at[d],
                send_sem=dem_send.at[d],
                recv_sem=dem_recv.at[d],
                device_id=downs[d],
                device_id_type=MESH,
            )
            move_dem[d].start()

    for d in near:
        move_emb[d].wait_recv()

    def phase_near():
        reward(near)

    phase_near()
    for d in distant:
        move_emb[d].wait_recv()

    def phase_distant():
        reward(distant)
        gradient(distant)

    phase_distant()
    send_back(distant)

    def phase_nearback():
        gradient(near)

    phase_nearback()
    send_back(reversed(near))
    for d in order:
        move_sco[d] = pltpu.make_async_remote_copy(
            src_ref=ssend.at[d],
            dst_ref=srecv.at[d],
            send_sem=sco_send.at[d],
            recv_sem=sco_recv.at[d],
            device_id=downs[d],
            device_id_type=MESH,
        )
        move_sco[d].start()

    for d in order:
        move_dem[d].wait_recv()
    demb = drecv[0].astype(F32)
    for d in range(1, slices):
        demb = demb + drecv[d].astype(F32)
    emb32[...] = demb

    def phase_da0():
        for f in range(2):
            for j in range(SUB):
                part = slice(j * channels, (j + 1) * channels)
                spread = jnp.concatenate(
                    [
                        jnp.broadcast_to(
                            emb32[p * slots + f * SUB + j : p * slots + f * SUB + j + 1, :],
                            (span, channels),
                        )
                        for p in range(REGIONS)
                    ],
                    axis=0,
                )
                da1[f * TPF : (f + 1) * TPF, part] = (
                    spread * a1[f * TPF : (f + 1) * TPF, part]
                ).astype(BF16)
            dfeat = dot_nt(da1[f * TPF : (f + 1) * TPF, :], up[...])
            part = slice(f * channels, (f + 1) * channels)
            da0[:, part] = (dfeat * a0[:, part]).astype(BF16)

    phase_da0()

    def phase_hsend():
        hsend[...] = dot_nt(da0[...], conv[0 : 2 * patch, :]).astype(BF16)

    phase_hsend()
    move_h = far(hsend, hrecv, 1, before)

    @pl.when(has_before)
    def _():
        move_h.start()

    own = dot_nt(da0[...], conv[2 * patch :, :])

    for d in order:
        move_sco[d].wait_recv()
    total = srecv[0]
    for d in range(1, slices):
        total = total + srecv[d]
    total = jnp.sum(total, axis=1, keepdims=True) / REGIONS
    index = lax.broadcasted_iota(jnp.int32, (slots, 128), 0)
    where = index + ctx * slots
    keep = ((where == 0) | (where >= SUB)) & (index == lane_at((slots, 128)))
    reward_out[...] = jnp.sum(jnp.where(keep, total, 0.0), axis=0, keepdims=True)

    @pl.when(has_after)
    def _():
        move_h.wait_recv()

    def phase_final():
        grad = (-sigma) * (own + hrecv[...].astype(F32))
        lean = (rstd[...] * grad).astype(BF16).astype(F32)
        one = lane_sums(lean * head_sums, each_half) / full
        two = lane_sums(lean * vel0[...], each_half) / full
        slope = rstd[...] * two
        offset = slope * mean[...] - one
        high = offset.astype(BF16).astype(F32)
        middle = (offset - high).astype(BF16).astype(F32)
        low = offset - high - middle
        nth = lax.rem(lane_at((TPF, lanes)), patch)
        tail = jnp.where(nth == 0, high, jnp.where(nth == 1, middle, low))
        tail = jnp.where(nth < 3, tail, 0.0)
        other = pltpu.roll(slope, patch, 1)
        lhs_out[0:TPF, :] = jnp.where(left, lean, pltpu.roll(tail, patch, 1)).astype(BF16)
        lhs_out[TPF:, :] = jnp.where(left, pltpu.roll(lean, patch, 1), tail).astype(BF16)
        coef_out[0:TPF, :] = jnp.where(left, slope, other)
        coef_out[TPF:, :] = jnp.where(left, other, slope)

    phase_final()

    @pl.when(has_after)
    def _():
        move_x.wait_send()

    @pl.when(has_before)
    def _():
        move_h.wait_send()

    for move in share_pair + share_twin + share_on:
        move.wait_send()
    for d in order:
        move_emb[d].wait_send()
        move_dem[d].wait_send()
        move_sco[d].wait_send()


def tail_kernel(hid, wide, lhs, coef, rewards, grad, reward_out, held, held_rewards, sem):
    chunks, tokens, width = hid.shape
    lanes = coef.shape[1]
    piece = width // 2
    block = 16
    held_rewards[...] = rewards[:, : held_rewards.shape[1]]
    copies = [pltpu.make_async_copy(held_rewards, reward_out, sem.at[0])]
    copies[0].start()
    for k in range(chunks):
        for begin in range(0, width, piece):
            product = dot_nn(lhs[...], wide[k, :, begin : begin + piece])
            first = k * width + begin
            for r in range(0, tokens, block):
                part = slice(r, r + block)
                slope = coef[part, :]
                for c in range(0, piece, lanes):
                    value = hid[k, part, begin + c : begin + c + lanes].astype(F32)
                    held[part, first + c : first + c + lanes] = (
                        product[part, c : c + lanes] - value * slope
                    ).astype(BF16)
            columns = pl.ds(first, piece)
            copy = pltpu.make_async_copy(
                held.at[:, columns], grad.at[:, columns], sem.at[len(copies)]
            )
            copy.start()
            copies.append(copy)
    for copy in copies:
        copy.wait()


def per_device(
    hidden,
    modulation,
    head_weight,
    noisy,
    timestep,
    conv_weight,
    up_weight,
    patch_proj,
    fc1,
    reward_vec,
):
    states = hidden[0]
    tokens, full = states.shape
    patch = head_weight.shape[0]
    channels = up_weight.shape[1]
    features_r, shard = fc1.shape
    slices = 4
    rows = 2 * SUB * REGIONS
    slots = 2 * SUB
    lanes = 2 * patch
    width = 1024
    chunks = full // width
    vmem = pltpu.VMEM

    scratch = [
        vmem((2, full), F32),
        vmem((patch, full), BF16),
        vmem((patch, tokens), BF16),
        vmem((4 * patch, 2 * channels), BF16),
        vmem((channels, SUB * channels), BF16),
        vmem((channels + 16, features_r), BF16),
        vmem((shard + 16, features_r), BF16),
        vmem((4 * shard + 2 * channels, channels), BF16),
        vmem((4, 8, shard), F32),
        vmem((1, shard), BF16),
        vmem((tokens, lanes), F32),
        vmem((tokens, lanes), F32),
        vmem((tokens, lanes), F32),
        vmem((patch, lanes), F32),
        vmem((patch, lanes), F32),
        vmem((TPF, lanes), F32),
        vmem((TPF, lanes), F32),
        vmem((TPF, lanes), F32),
        vmem((TPF, lanes), F32),
        vmem((TPF, lanes), BF16),
        vmem((TPF, lanes), BF16),
        vmem((TPF, 2 * channels), F32),
        vmem((tokens, channels), BF16),
        vmem((tokens, SUB * channels), F32),
        vmem((rows, channels), F32),
        vmem((rows, channels), BF16),
        vmem((slices, rows, channels), BF16),
        vmem((slices * rows, 4 * shard + 2 * channels), F32),
        vmem((slices * rows, 128), F32),
        vmem((slices * rows, 4 * shard), BF16),
        vmem((slices, rows, channels), BF16),
        vmem((slices, rows, channels), BF16),
        vmem((slices, slots, 128), F32),
        vmem((slices, slots, 128), F32),
        vmem((tokens, SUB * channels), BF16),
        vmem((TPF, 2 * channels), BF16),
        vmem((TPF, lanes), BF16),
        vmem((TPF, lanes), BF16),
        pltpu.SemaphoreType.DMA((chunks,)),
        pltpu.SemaphoreType.DMA((20,)),
        pltpu.SemaphoreType.DMA((8,)),
        pltpu.SemaphoreType.DMA((8,)),
        pltpu.SemaphoreType.DMA((slices,)),
        pltpu.SemaphoreType.DMA((slices,)),
        pltpu.SemaphoreType.DMA((slices,)),
        pltpu.SemaphoreType.DMA((slices,)),
        pltpu.SemaphoreType.DMA((slices,)),
        pltpu.SemaphoreType.DMA((slices,)),
    ]
    in_hbm = pl.BlockSpec(memory_space=pltpu.HBM)
    local = pl.BlockSpec(memory_space=pltpu.VMEM)
    hid, wide, lhs, coef, rewards = pl.pallas_call(
        main_kernel,
        out_shape=(
            vmem((chunks, tokens, width), BF16),
            vmem((chunks, lanes, width), BF16),
            vmem((tokens, lanes), BF16),
            vmem((tokens, lanes), F32),
            vmem((1, 128), F32),
        ),
        in_specs=[pl.BlockSpec(memory_space=pltpu.SMEM)] + [in_hbm] * 9,
        out_specs=(local,) * 5,
        scratch_shapes=scratch,
        compiler_params=pltpu.CompilerParams(
            collective_id=0, has_side_effects=True, vmem_limit_bytes=36 * 1024 * 1024
        ),
        name="reward_step",
    )(
        timestep,
        *(
            pltpu.with_memory_space_constraint(value, pltpu.HBM)
            for value in (
                states,
                modulation,
                head_weight,
                noisy[0].T,
                conv_weight,
                up_weight,
                patch_proj,
                fc1.T,
                reward_vec,
            )
        ),
    )
    grad, reward = pl.pallas_call(
        tail_kernel,
        out_shape=(
            jax.ShapeDtypeStruct((tokens, full), BF16),
            jax.ShapeDtypeStruct((1, slots), F32),
        ),
        in_specs=[local] * 5,
        out_specs=(in_hbm, in_hbm),
        scratch_shapes=[
            vmem((tokens, full), BF16),
            vmem((1, slots), F32),
            pltpu.SemaphoreType.DMA((2 * chunks + 1,)),
        ],
        compiler_params=pltpu.CompilerParams(vmem_limit_bytes=20 * 1024 * 1024),
        name="hidden_gradient",
    )(hid, wide, lhs, coef, rewards)
    return (grad[None], reward)


def solution(mesh):
    return jax.shard_map(
        per_device,
        mesh=mesh,
        in_specs=(
            P("fsdp", "ctx", None),
            P(),
            P(),
            P("fsdp", "ctx", None),
            P(),
            P(),
            P(),
            P(),
            P(None, "fsdp"),
            P(None, "fsdp"),
        ),
        out_specs=(P("fsdp", "ctx", None), P("fsdp", "ctx")),
        check_vma=False,
    )
```

```python
import jax
import jax.numpy as jnp
from jax import lax
from jax.experimental import pallas as pl
from jax.experimental.pallas import tpu as pltpu
from jax.sharding import PartitionSpec as P

TPF = 224
REGIONS = 4
SUB = 4
LOSS_WEIGHT = 65536.0
EPSILON = 1e-06
F32 = jnp.float32
BF16 = jnp.bfloat16
MESH = pl.DeviceIdType.MESH


def dot_nn(a, b):
    return lax.dot_general(a, b, (((1,), (0,)), ((), ())), preferred_element_type=F32)


def dot_nt(a, b):
    return lax.dot_general(a, b, (((1,), (1,)), ((), ())), preferred_element_type=F32)


def sigmoid(value):
    return 0.5 + 0.5 * jnp.tanh(0.5 * value)


def silu(value):
    half = 0.5 * value
    return half + half * jnp.tanh(half)


def silu_slope(value):
    half = 0.5 * value
    tangent = jnp.tanh(half)
    return (0.5 + 0.5 * tangent) * (1.0 + half * (1.0 - tangent))


def two_parts(value):
    high = value.astype(BF16)
    return [high, (value - high.astype(F32)).astype(BF16)]


def lane_sums(values, patterns):
    parts = [part for value in values for part in two_parts(value)]
    rows = [pattern for pattern in patterns for _ in range(2)]
    return dot_nn(jnp.concatenate(parts, axis=1), jnp.concatenate(rows, axis=0))


def main_kernel(
    timestep,
    hidden,
    modulation,
    head_weight,
    noisy_t,
    conv_weight,
    up_weight,
    patch_proj,
    fc1_t,
    reward_vec,
    hid,
    wide,
    lhs_out,
    coef_out,
    reward_out,
    mod,
    head,
    noisy,
    conv,
    up,
    proj,
    cols,
    mixed,
    vec,
    vec_in,
    acc,
    ssq,
    pilot,
    sums_part,
    shift_part,
    latents,
    vel0,
    rstd,
    mean,
    xown,
    xhalo,
    a0,
    feat,
    a1,
    emb32,
    emb,
    eall,
    terms,
    factors,
    g,
    dsend,
    drecv,
    ssend,
    srecv,
    da1,
    da0,
    hsend,
    hrecv,
    hid_sem,
    in_sem,
    far_send,
    far_recv,
    emb_send,
    emb_recv,
    dem_send,
    dem_recv,
    sco_send,
    sco_recv,
):
    chunks, tokens, width = hid.shape
    full = chunks * width
    patch = head.shape[0]
    lanes = 2 * patch
    channels = up.shape[0]
    features_r = proj.shape[1]
    shard = fc1_t.shape[0]
    span = TPF // REGIONS
    rows = eall.shape[1]
    slices = eall.shape[0]
    spots = lax.axis_size("fsdp") // 2
    slots = 2 * SUB
    block = 16

    ctx, fsdp = lax.axis_index("ctx"), lax.axis_index("fsdp")
    steps = lax.axis_size("ctx")
    z, core = fsdp // 2, fsdp % 2
    after = (lax.rem(ctx + 1, steps), fsdp)
    before = (lax.rem(ctx + steps - 1, steps), fsdp)
    twin = (ctx, z * 2 + 1 - core)
    side = 1 - 2 * lax.rem(z, 2)

    def chip(offset):
        return lax.rem(z + offset * side + spots, spots)

    def other_core(offset):
        return (ctx, chip(offset) * 2 + 1 - core)

    def turn(spot):
        return jnp.where(spot >= spots // 2, 1, 0)

    pair = (ctx, (z + side) * 2 + core)
    reach = [other_core(offset) for offset in (0, -1, -2, -3, 2)] + [pair]
    has_before, has_after = ctx > 0, ctx < steps - 1

    loads = []

    def load(source, target):
        copy = pltpu.make_async_copy(source, target, in_sem.at[len(loads)])
        copy.start()
        loads.append(copy)
        return copy

    load_proj = load(patch_proj, proj.at[pl.ds(0, channels)])
    load_cols = load(fc1_t, cols.at[pl.ds(0, shard)])
    load_mod = load(modulation, mod)
    load_head = load(head_weight, head)
    hid_loads = []
    for k in range(chunks):
        copy = pltpu.make_async_copy(
            hidden.at[:, pl.ds(k * width, width)], hid.at[k], hid_sem.at[k]
        )
        copy.start()
        hid_loads.append(copy)

    barrier = pltpu.get_barrier_semaphore()
    for peer in reach:
        pl.semaphore_signal(barrier, inc=1, device_id=peer, device_id_type=MESH)

    @pl.when(has_after)
    def _():
        pl.semaphore_signal(barrier, inc=1, device_id=after, device_id_type=MESH)

    @pl.when(has_before)
    def _():
        pl.semaphore_signal(barrier, inc=1, device_id=before, device_id_type=MESH)

    load_noisy = load(noisy_t, noisy)
    load_vec = load(reward_vec, vec_in)
    load_conv = []
    for frame in range(2):
        for lag in range(3):
            spot = frame + 2 - lag
            load_conv.append(
                load(
                    conv_weight.at[lag],
                    conv.at[pl.ds(spot * patch, patch), pl.ds(frame * channels, channels)],
                )
            )
    load_up = [
        load(up_weight.at[j], up.at[:, pl.ds(j * channels, channels)]) for j in range(SUB)
    ]

    proj[channels:, :] = jnp.ones((proj.shape[0] - channels, features_r), BF16)
    cols[shard:, :] = jnp.ones((cols.shape[0] - shard, features_r), BF16)

    @pl.when(jnp.logical_not(has_before))
    def _():
        xhalo[...] = jnp.zeros_like(xhalo)

    @pl.when(jnp.logical_not(has_after))
    def _():
        hrecv[...] = jnp.zeros_like(hrecv)

    empty = jnp.zeros((patch, channels), BF16)
    conv[0:patch, channels:] = empty
    conv[3 * patch :, :channels] = empty
    for k in range(chunks):
        wide[k, patch:, :] = jnp.ones((patch, width), BF16)

    def lane_at(shape):
        return lax.broadcasted_iota(jnp.int32, shape, 1)

    left = lane_at((TPF, lanes)) < patch
    row_id = lax.broadcasted_iota(jnp.int32, (lanes, lanes), 0)
    col_id = lane_at((lanes, lanes))
    to_left = jnp.where(col_id < patch, 1.0, 0.0).astype(BF16)
    to_right = jnp.where(col_id < patch, 0.0, 1.0).astype(BF16)
    each_half = jnp.where((row_id < patch) == (col_id < patch), 1.0, 0.0).astype(BF16)
    nothing = jnp.zeros((lanes, lanes), BF16)

    def prepare():
        for r in range(0, patch, block):
            part = slice(r, r + block)
            cs = jnp.zeros((block, lanes), F32)
            bw = jnp.zeros((block, lanes), F32)
            for c in range(0, full, lanes):
                columns = slice(c, c + lanes)
                plain = head[part, columns].astype(F32)
                scaled = (plain * (1.0 + mod[1:2, columns])).astype(BF16)
                wide[c // width, part, c % width : c % width + lanes] = scaled
                cs = cs + scaled.astype(F32)
                bw = bw + plain * mod[0:1, columns]
            sums_part[part, :], shift_part[part, :] = cs, bw

    def features(group):
        first = group[0] == 0
        product = dot_nt(hid[group[0]], wide[group[0]])
        for k in group[1:]:
            product = product + dot_nt(hid[k], wide[k])
        acc[...] = product if first else acc[...] + product
        for r in range(0, tokens, block):
            part = slice(r, r + block)
            centre = pilot[part, :]
            total = jnp.zeros((block, lanes), F32) if first else ssq[part, :]
            for k in group:
                for c in range(0, width, lanes):
                    value = hid[k, part, c : c + lanes].astype(F32) - centre
                    total = total + value * value
            ssq[part, :] = total

    def phase_mixed():
        product = dot_nt(cols[...], proj[...])
        centre = product[shard : shard + 1, 0:channels] * (1.0 / features_r)
        mixed[0:shard, :] = (
            product[0:shard, 0:channels] - product[0:shard, channels : channels + 1] * centre
        ).astype(BF16)

    def phase_gram():
        product = dot_nt(proj[...], proj[...]) * (1.0 / features_r)
        centre = product[0:channels, channels : channels + 1]
        gram = product[0:channels, 0:channels] - centre * product[channels : channels + 1, 0:channels]
        high = gram.astype(BF16)
        mixed[4 * shard : 4 * shard + channels, :] = high
        mixed[4 * shard + channels :, :] = (gram - high.astype(F32)).astype(BF16)

    def column_sums(values):
        pieces = []
        for value in values:
            high, rest = two_parts(value)
            low = (value - high.astype(F32) - rest.astype(F32)).astype(BF16)
            pieces += [jnp.concatenate([high, rest, low], axis=1)] * 2
        return dot_nt(jnp.ones((8, 3 * lanes), BF16), jnp.concatenate(pieces, axis=0))[0:1, :]

    def far(source, target, index, device):
        return pltpu.make_async_remote_copy(
            src_ref=source,
            dst_ref=target,
            send_sem=far_send.at[index],
            recv_sem=far_recv.at[index],
            device_id=device,
            device_id_type=MESH,
        )

    def share(index, source, target, device):
        moves = [
            far(
                mixed.at[pl.ds(source * shard, shard)],
                mixed.at[pl.ds(target * shard, shard)],
                index,
                device,
            ),
            far(vec.at[source], vec.at[target], index + 1, device),
        ]
        for move in moves:
            move.start()
        return moves

    load_proj.wait()
    load_cols.wait()
    phase_mixed()
    load_vec.wait()
    vec[0] = jnp.broadcast_to(vec_in[...].astype(F32), vec.shape[1:])
    load_mod.wait()
    load_head.wait()
    prepare()
    sums = column_sums([sums_part[...], shift_part[...]])
    head_sums, head_shift = sums[:, 0:lanes], sums[:, lanes:]
    hid_loads[0].wait()
    pilot[...] = jnp.broadcast_to(hid[0, :, 0:1].astype(F32), pilot.shape)
    groups = [[0]] + [list(range(k, min(k + 2, chunks))) for k in range(1, chunks, 2)]
    for group in groups:
        for k in group:
            if k > 0:
                hid_loads[k].wait()
        if group is groups[-1]:
            load_noisy.wait()
            token = lax.broadcasted_iota(jnp.int32, (TPF, 2 * TPF), 0)
            place = lane_at((TPF, 2 * TPF))
            pick = jnp.concatenate([place == token, place == token + TPF], axis=0)
            both = dot_nt(jnp.where(pick, 1.0, 0.0).astype(BF16), noisy[...])
            pair_rows = jnp.concatenate([both[0:TPF], both[TPF:]], axis=1)
            latents[...] = pair_rows
        features(group)
        if group is groups[0]:
            reached = len(reach) + jnp.where(has_before, 1, 0) + jnp.where(has_after, 1, 0)
            pl.semaphore_wait(barrier, reached)
            share_pair = share(2, 0, 1, pair)
            share_twin = share(4, 0, 2, twin)
    step_frac = jnp.full((1, lanes), timestep[0].astype(F32)) / 1000.0
    sigma = 5.0 * step_frac / (1.0 + 4.0 * step_frac)

    def phase_latents():
        one, two = acc[0:TPF, :], acc[TPF:, :]
        average = jnp.where(left, pltpu.roll(one, patch, 1), two) * (1.0 / full)
        product = jnp.where(left, one, pltpu.roll(two, patch, 1))
        off = average - jnp.where(left, pilot[0:TPF, :], pilot[TPF:, :])
        square = lane_sums([ssq[0:TPF, :], ssq[TPF:, :]], [to_left, to_right])
        var = jnp.maximum(square * (1.0 / full) - off * off, 0.0)
        scale = lax.rsqrt(var + EPSILON)
        mean[...] = average
        rstd[...] = scale
        velocity = scale * (product - average * head_sums)
        vel0[...] = velocity
        xown[...] = (latents[...] - sigma * (velocity + head_shift)).astype(BF16)

    phase_latents()

    move_x = far(xown, xhalo, 0, after)

    @pl.when(has_after)
    def _():
        move_x.start()

    phase_gram()
    for copy in load_conv + load_up:
        copy.wait()
    a0[...] = dot_nn(xown[...], conv[2 * patch :, :])

    @pl.when(has_before)
    def _():
        move_x.wait_recv()

    def phase_feat():
        a0[...] += dot_nn(xhalo[...], conv[0 : 2 * patch, :])
        for f in range(2):
            for r in range(0, TPF, block):
                value = a0[r : r + block, f * channels : (f + 1) * channels]
                feat[f * TPF + r : f * TPF + r + block, :] = silu(value).astype(BF16)

    phase_feat()

    def phase_upsample():
        for j in range(SUB):
            part = slice(j * channels, (j + 1) * channels)
            a1[:, part] = dot_nn(feat[...], up[:, part])
            for f in range(2):
                for p in range(REGIONS):
                    begin = f * TPF + p * span
                    pooled = jnp.sum(
                        silu(a1[begin : begin + span, part]), axis=0, keepdims=True
                    )
                    row = p * slots + f * SUB + j
                    emb32[row : row + 1, :] = pooled * (1.0 / span)

    phase_upsample()
    emb[...] = emb32[...].astype(BF16)

    order = list(range(slices - 1, -1, -1))
    line = list(range(slices))
    first_half, second_half = line[:2], line[2:]

    def send_emb(q, place, device):
        return pltpu.make_async_remote_copy(
            src_ref=emb,
            dst_ref=eall.at[place],
            send_sem=emb_send.at[q],
            recv_sem=emb_recv.at[place],
            device_id=device,
            device_id_type=MESH,
        )

    move_emb = {}
    for q, offset in ((3, -3), (2, 2), (1, -1), (0, 0)):
        place = lax.rem(q + turn(chip(offset)), slices)
        move_emb[q] = send_emb(q, place, other_core(offset))
        move_emb[q].start()

    for move in share_pair:
        move.wait_recv()
    share_on = share(6, 1, 3, twin)

    def phase_slopes():
        for f in range(2):
            for r in range(0, TPF, block):
                for j in range(SUB):
                    part = slice(j * channels, (j + 1) * channels)
                    where = slice(f * TPF + r, f * TPF + r + block)
                    a1[where, part] = silu_slope(a1[where, part])
                part = slice(f * channels, (f + 1) * channels)
                a0[r : r + block, part] = silu_slope(a0[r : r + block, part])

    phase_slopes()
    for move in share_twin + share_on:
        move.wait_recv()
    weight = jnp.concatenate([vec[q] for q in range(4)], axis=1)[0:1, :]
    slot = lax.rem(lax.broadcasted_iota(jnp.int32, (rows, 1), 0), slots) + ctx * slots
    present = jnp.where((slot == 0) | (slot >= SUB), 1.0, 0.0)
    row_scale = present * (-LOSS_WEIGHT / REGIONS / span)

    def row_of(d):
        return line.index(d) * rows

    def all_rows(group):
        return slice(row_of(group[0]), row_of(group[-1]) + rows)

    def reward(group):
        part = all_rows(group)
        both = 4 * shard
        terms[part, :] = dot_nt(
            jnp.concatenate([eall[d] for d in group], axis=0), mixed[...]
        )
        coeff = 0.7978845608028654
        for d in group:
            total = None
            for r in range(0, rows, block):
                where = slice(row_of(d) + r, row_of(d) + r + block)
                pulled = terms[where, both : both + channels] + terms[where, both + channels :]
                own_emb = eall[d, r : r + block, :].astype(F32)
                var = jnp.sum(pulled * own_emb, axis=1, keepdims=True)
                scale = lax.rsqrt(jnp.maximum(var, 0.0) + EPSILON)
                value = terms[where, :both] * scale
                square = value * value
                tangent = jnp.tanh(value * (coeff + (coeff * 0.044715) * square))
                half = 0.5 * (1.0 + tangent)
                slope = half + 0.5 * value * (1.0 - tangent * tangent) * (
                    coeff + (coeff * 3.0 * 0.044715) * square
                )
                slope = (weight * slope).astype(BF16)
                g[where, :] = slope
                along = jnp.sum(slope.astype(F32) * value, axis=1, keepdims=True)
                factor = scale * row_scale[r : r + block]
                factors[where, :] = jnp.broadcast_to(factor, (block, 128))
                terms[where, both : both + channels] = pulled * (factor * scale * along)
                points = value * half * weight
                for q in range(0, block, slots):
                    for c in range(0, both, 128):
                        piece = points[q : q + slots, c : c + 128]
                        total = piece if total is None else total + piece
            ssend[d] = total

    def gradient(group):
        part = all_rows(group)
        both = 4 * shard
        back = dot_nn(g[part, :], mixed[0:both, :])
        for d in group:
            where = slice(row_of(d), row_of(d) + rows)
            begin = row_of(d) - part.start
            dsend[d] = (
                back[begin : begin + rows] * factors[where, 0:1]
                - terms[where, both : both + channels]
            ).astype(BF16)

    def give_back(source, target, send_sem, recv_sem, p):
        q = lax.rem(p + slices - turn(z), slices)
        return pltpu.make_async_remote_copy(
            src_ref=source.at[p],
            dst_ref=target.at[q],
            send_sem=send_sem.at[p],
            recv_sem=recv_sem.at[q],
            device_id=other_core(-q),
            device_id_type=MESH,
        )

    def arrival(source, target, send_sem, recv_sem, q):
        return pltpu.make_async_remote_copy(
            src_ref=source.at[q],
            dst_ref=target.at[q],
            send_sem=send_sem.at[q],
            recv_sem=recv_sem.at[q],
            device_id=twin,
            device_id_type=MESH,
        )

    back_refs = (dsend, drecv, dem_send, dem_recv)
    score_refs = (ssend, srecv, sco_send, sco_recv)
    move_dem, move_sco = {}, {}

    def serve(group):
        for p in group:
            send_emb(0, p, twin).wait_recv()
        reward(group)
        gradient(group)
        for p in group:
            move_dem[p] = give_back(*back_refs, p)
            move_dem[p].start()

    serve(first_half)
    serve(second_half)
    for p in line:
        move_sco[p] = give_back(*score_refs, p)
        move_sco[p].start()

    for q in line:
        arrival(*back_refs, q).wait_recv()
    demb = drecv[0].astype(F32)
    for d in range(1, slices):
        demb = demb + drecv[d].astype(F32)
    emb32[...] = demb

    def phase_da0():
        for f in range(2):
            for j in range(SUB):
                part = slice(j * channels, (j + 1) * channels)
                spread = jnp.concatenate(
                    [
                        jnp.broadcast_to(
                            emb32[p * slots + f * SUB + j : p * slots + f * SUB + j + 1, :],
                            (span, channels),
                        )
                        for p in range(REGIONS)
                    ],
                    axis=0,
                )
                da1[f * TPF : (f + 1) * TPF, part] = (
                    spread * a1[f * TPF : (f + 1) * TPF, part]
                ).astype(BF16)
            dfeat = dot_nt(da1[f * TPF : (f + 1) * TPF, :], up[...])
            part = slice(f * channels, (f + 1) * channels)
            da0[:, part] = (dfeat * a0[:, part]).astype(BF16)

    phase_da0()

    def phase_hsend():
        hsend[...] = dot_nt(da0[...], conv[0 : 2 * patch, :]).astype(BF16)

    phase_hsend()
    move_h = far(hsend, hrecv, 1, before)

    @pl.when(has_before)
    def _():
        move_h.start()

    own = dot_nt(da0[...], conv[2 * patch :, :])

    for d in order:
        arrival(*score_refs, d).wait_recv()
    total = srecv[0]
    for d in range(1, slices):
        total = total + srecv[d]
    total = jnp.sum(total, axis=1, keepdims=True) / REGIONS
    index = lax.broadcasted_iota(jnp.int32, (slots, 128), 0)
    where = index + ctx * slots
    keep = ((where == 0) | (where >= SUB)) & (index == lane_at((slots, 128)))
    reward_out[...] = jnp.sum(jnp.where(keep, total, 0.0), axis=0, keepdims=True)

    @pl.when(has_after)
    def _():
        move_h.wait_recv()

    def phase_final():
        grad = (-sigma) * (own + hrecv[...].astype(F32))
        lean = (rstd[...] * grad).astype(BF16).astype(F32)
        means = lane_sums(
            [lean * head_sums, lean * vel0[...]],
            [
                jnp.concatenate([each_half, nothing], axis=1),
                jnp.concatenate([nothing, each_half], axis=1),
            ],
        ) * (1.0 / full)
        one = means[:, 0:lanes]
        slope = rstd[...] * means[:, lanes:]
        offset = slope * mean[...] - one
        high = offset.astype(BF16).astype(F32)
        middle = (offset - high).astype(BF16).astype(F32)
        low = offset - high - middle
        nth = lax.rem(lane_at((TPF, lanes)), patch)
        tail = jnp.where(nth == 0, high, jnp.where(nth == 1, middle, low))
        tail = jnp.where(nth < 3, tail, 0.0)
        other = pltpu.roll(slope, patch, 1)
        lhs_out[0:TPF, :] = jnp.where(left, lean, pltpu.roll(tail, patch, 1)).astype(BF16)
        lhs_out[TPF:, :] = jnp.where(left, pltpu.roll(lean, patch, 1), tail).astype(BF16)
        coef_out[0:TPF, :] = jnp.where(left, slope, other)
        coef_out[TPF:, :] = jnp.where(left, other, slope)

    phase_final()

    @pl.when(has_after)
    def _():
        move_x.wait_send()

    @pl.when(has_before)
    def _():
        move_h.wait_send()

    for move in share_pair + share_twin + share_on:
        move.wait_send()
    for d in order:
        move_emb[d].wait_send()
        move_dem[d].wait_send()
        move_sco[d].wait_send()


def tail_kernel(hid, wide, lhs, coef, rewards, grad, reward_out, held, held_rewards, sem):
    chunks, tokens, width = hid.shape
    lanes = coef.shape[1]
    piece = width // 2
    block = 16
    held_rewards[...] = rewards[:, : held_rewards.shape[1]]
    copies = [pltpu.make_async_copy(held_rewards, reward_out, sem.at[0])]
    copies[0].start()
    for k in range(chunks):
        for begin in range(0, width, piece):
            product = dot_nn(lhs[...], wide[k, :, begin : begin + piece])
            first = k * width + begin
            for r in range(0, tokens, block):
                part = slice(r, r + block)
                slope = coef[part, :]
                for c in range(0, piece, lanes):
                    value = hid[k, part, begin + c : begin + c + lanes].astype(F32)
                    held[part, first + c : first + c + lanes] = (
                        product[part, c : c + lanes] - value * slope
                    ).astype(BF16)
            columns = pl.ds(first, piece)
            copy = pltpu.make_async_copy(
                held.at[:, columns], grad.at[:, columns], sem.at[len(copies)]
            )
            copy.start()
            copies.append(copy)
    for copy in copies:
        copy.wait()


def per_device(
    hidden,
    modulation,
    head_weight,
    noisy,
    timestep,
    conv_weight,
    up_weight,
    patch_proj,
    fc1,
    reward_vec,
):
    states = hidden[0]
    tokens, full = states.shape
    patch = head_weight.shape[0]
    channels = up_weight.shape[1]
    features_r, shard = fc1.shape
    slices = 4
    rows = 2 * SUB * REGIONS
    slots = 2 * SUB
    lanes = 2 * patch
    width = 1024
    chunks = full // width
    vmem = pltpu.VMEM

    scratch = [
        vmem((2, full), F32),
        vmem((patch, full), BF16),
        vmem((patch, tokens), BF16),
        vmem((4 * patch, 2 * channels), BF16),
        vmem((channels, SUB * channels), BF16),
        vmem((channels + 16, features_r), BF16),
        vmem((shard + 16, features_r), BF16),
        vmem((4 * shard + 2 * channels, channels), BF16),
        vmem((4, 8, shard), F32),
        vmem((1, shard), BF16),
        vmem((tokens, lanes), F32),
        vmem((tokens, lanes), F32),
        vmem((tokens, lanes), F32),
        vmem((patch, lanes), F32),
        vmem((patch, lanes), F32),
        vmem((TPF, lanes), F32),
        vmem((TPF, lanes), F32),
        vmem((TPF, lanes), F32),
        vmem((TPF, lanes), F32),
        vmem((TPF, lanes), BF16),
        vmem((TPF, lanes), BF16),
        vmem((TPF, 2 * channels), F32),
        vmem((tokens, channels), BF16),
        vmem((tokens, SUB * channels), F32),
        vmem((rows, channels), F32),
        vmem((rows, channels), BF16),
        vmem((slices, rows, channels), BF16),
        vmem((slices * rows, 4 * shard + 2 * channels), F32),
        vmem((slices * rows, 128), F32),
        vmem((slices * rows, 4 * shard), BF16),
        vmem((slices, rows, channels), BF16),
        vmem((slices, rows, channels), BF16),
        vmem((slices, slots, 128), F32),
        vmem((slices, slots, 128), F32),
        vmem((tokens, SUB * channels), BF16),
        vmem((TPF, 2 * channels), BF16),
        vmem((TPF, lanes), BF16),
        vmem((TPF, lanes), BF16),
        pltpu.SemaphoreType.DMA((chunks,)),
        pltpu.SemaphoreType.DMA((20,)),
        pltpu.SemaphoreType.DMA((8,)),
        pltpu.SemaphoreType.DMA((8,)),
        pltpu.SemaphoreType.DMA((slices,)),
        pltpu.SemaphoreType.DMA((slices,)),
        pltpu.SemaphoreType.DMA((slices,)),
        pltpu.SemaphoreType.DMA((slices,)),
        pltpu.SemaphoreType.DMA((slices,)),
        pltpu.SemaphoreType.DMA((slices,)),
    ]
    in_hbm = pl.BlockSpec(memory_space=pltpu.HBM)
    local = pl.BlockSpec(memory_space=pltpu.VMEM)
    hid, wide, lhs, coef, rewards = pl.pallas_call(
        main_kernel,
        out_shape=(
            vmem((chunks, tokens, width), BF16),
            vmem((chunks, lanes, width), BF16),
            vmem((tokens, lanes), BF16),
            vmem((tokens, lanes), F32),
            vmem((1, 128), F32),
        ),
        in_specs=[pl.BlockSpec(memory_space=pltpu.SMEM)] + [in_hbm] * 9,
        out_specs=(local,) * 5,
        scratch_shapes=scratch,
        compiler_params=pltpu.CompilerParams(
            collective_id=0, has_side_effects=True, vmem_limit_bytes=36 * 1024 * 1024
        ),
        name="reward_step",
    )(
        timestep,
        *(
            pltpu.with_memory_space_constraint(value, pltpu.HBM)
            for value in (
                states,
                modulation,
                head_weight,
                noisy[0].T,
                conv_weight,
                up_weight,
                patch_proj,
                fc1.T,
                reward_vec,
            )
        ),
    )
    grad, reward = pl.pallas_call(
        tail_kernel,
        out_shape=(
            jax.ShapeDtypeStruct((tokens, full), BF16),
            jax.ShapeDtypeStruct((1, slots), F32),
        ),
        in_specs=[local] * 5,
        out_specs=(in_hbm, in_hbm),
        scratch_shapes=[
            vmem((tokens, full), BF16),
            vmem((1, slots), F32),
            pltpu.SemaphoreType.DMA((2 * chunks + 1,)),
        ],
        compiler_params=pltpu.CompilerParams(vmem_limit_bytes=20 * 1024 * 1024),
        name="hidden_gradient",
    )(hid, wide, lhs, coef, rewards)
    return (grad[None], reward)


def solution(mesh):
    return jax.shard_map(
        per_device,
        mesh=mesh,
        in_specs=(
            P("fsdp", "ctx", None),
            P(),
            P(),
            P("fsdp", "ctx", None),
            P(),
            P(),
            P(),
            P(),
            P(None, "fsdp"),
            P(None, "fsdp"),
        ),
        out_specs=(P("fsdp", "ctx", None), P("fsdp", "ctx")),
        check_vma=False,
    )
```

```python
import jax
import jax.numpy as jnp
from jax import lax
from jax.experimental import pallas as pl
from jax.experimental.pallas import tpu as pltpu
from jax.sharding import PartitionSpec as P

TPF = 224
REGIONS = 4
SUB = 4
LOSS_WEIGHT = 65536.0
EPSILON = 1e-06
F32 = jnp.float32
BF16 = jnp.bfloat16
MESH = pl.DeviceIdType.MESH


def dot_nn(a, b):
    return lax.dot_general(a, b, (((1,), (0,)), ((), ())), preferred_element_type=F32)


def dot_nt(a, b):
    return lax.dot_general(a, b, (((1,), (1,)), ((), ())), preferred_element_type=F32)


def sigmoid(value):
    return 0.5 + 0.5 * jnp.tanh(0.5 * value)


def silu(value):
    half = 0.5 * value
    return half + half * jnp.tanh(half)


def silu_slope(value):
    half = 0.5 * value
    tangent = jnp.tanh(half)
    return (0.5 + 0.5 * tangent) * (1.0 + half * (1.0 - tangent))


def two_parts(value):
    high = value.astype(BF16)
    return [high, (value - high.astype(F32)).astype(BF16)]


def lane_sums(values, patterns):
    parts = [part for value in values for part in two_parts(value)]
    rows = [pattern for pattern in patterns for _ in range(2)]
    return dot_nn(jnp.concatenate(parts, axis=1), jnp.concatenate(rows, axis=0))


def main_kernel(
    timestep,
    hidden,
    modulation,
    head_weight,
    noisy_t,
    conv_weight,
    up_weight,
    patch_proj,
    fc1_t,
    reward_vec,
    hid,
    wide,
    lhs_out,
    coef_out,
    reward_out,
    mod,
    head,
    noisy,
    conv,
    up,
    proj,
    cols,
    mixed,
    vec,
    vec_in,
    acc,
    ssq,
    pilot,
    sums_part,
    shift_part,
    latents,
    vel0,
    rstd,
    mean,
    xown,
    xhalo,
    a0,
    feat,
    a1,
    emb32,
    emb,
    eall,
    terms,
    factors,
    g,
    dsend,
    drecv,
    ssend,
    srecv,
    da1,
    da0,
    hsend,
    hrecv,
    hid_sem,
    in_sem,
    far_send,
    far_recv,
    emb_send,
    emb_recv,
    dem_send,
    dem_recv,
    sco_send,
    sco_recv,
):
    chunks, tokens, width = hid.shape
    full = chunks * width
    patch = head.shape[0]
    lanes = 2 * patch
    channels = up.shape[0]
    features_r = proj.shape[1]
    shard = fc1_t.shape[0]
    span = TPF // REGIONS
    rows = eall.shape[1]
    slices = eall.shape[0]
    spots = lax.axis_size("fsdp") // 2
    slots = 2 * SUB
    block = 16

    ctx, fsdp = lax.axis_index("ctx"), lax.axis_index("fsdp")
    steps = lax.axis_size("ctx")
    z, core = fsdp // 2, fsdp % 2
    after = (lax.rem(ctx + 1, steps), fsdp)
    before = (lax.rem(ctx + steps - 1, steps), fsdp)
    twin = (ctx, z * 2 + 1 - core)
    side = 1 - 2 * lax.rem(z, 2)

    def chip(offset):
        return lax.rem(z + offset * side + spots, spots)

    def other_core(offset):
        return (ctx, chip(offset) * 2 + 1 - core)

    def turn(spot):
        return jnp.where(spot >= spots // 2, 1, 0)

    pair = (ctx, (z + side) * 2 + core)
    reach = [other_core(offset) for offset in (0, -1, -2, -3, 2)] + [pair]
    has_before, has_after = ctx > 0, ctx < steps - 1

    loads = []

    def load(source, target):
        copy = pltpu.make_async_copy(source, target, in_sem.at[len(loads)])
        copy.start()
        loads.append(copy)
        return copy

    load_mod = load(modulation, mod)
    load_head = load(head_weight, head)
    hid_loads = []
    for k in range(chunks):
        copy = pltpu.make_async_copy(
            hidden.at[:, pl.ds(k * width, width)], hid.at[k], hid_sem.at[k]
        )
        copy.start()
        hid_loads.append(copy)
    load_proj = load(patch_proj, proj.at[pl.ds(0, channels)])
    load_cols = load(fc1_t, cols.at[pl.ds(0, shard)])

    barrier = pltpu.get_barrier_semaphore()
    for peer in reach:
        pl.semaphore_signal(barrier, inc=1, device_id=peer, device_id_type=MESH)

    @pl.when(has_after)
    def _():
        pl.semaphore_signal(barrier, inc=1, device_id=after, device_id_type=MESH)

    @pl.when(has_before)
    def _():
        pl.semaphore_signal(barrier, inc=1, device_id=before, device_id_type=MESH)

    load_noisy = load(noisy_t, noisy)
    load_vec = load(reward_vec, vec_in)
    load_conv = []
    for frame in range(2):
        for lag in range(3):
            spot = frame + 2 - lag
            load_conv.append(
                load(
                    conv_weight.at[lag],
                    conv.at[pl.ds(spot * patch, patch), pl.ds(frame * channels, channels)],
                )
            )
    load_up = [
        load(up_weight.at[j], up.at[:, pl.ds(j * channels, channels)]) for j in range(SUB)
    ]

    proj[channels:, :] = jnp.ones((proj.shape[0] - channels, features_r), BF16)
    cols[shard:, :] = jnp.ones((cols.shape[0] - shard, features_r), BF16)

    @pl.when(jnp.logical_not(has_before))
    def _():
        xhalo[...] = jnp.zeros_like(xhalo)

    @pl.when(jnp.logical_not(has_after))
    def _():
        hrecv[...] = jnp.zeros_like(hrecv)

    empty = jnp.zeros((patch, channels), BF16)
    conv[0:patch, channels:] = empty
    conv[3 * patch :, :channels] = empty
    for k in range(chunks):
        wide[k, patch:, :] = jnp.ones((patch, width), BF16)

    def lane_at(shape):
        return lax.broadcasted_iota(jnp.int32, shape, 1)

    left = lane_at((TPF, lanes)) < patch
    row_id = lax.broadcasted_iota(jnp.int32, (lanes, lanes), 0)
    col_id = lane_at((lanes, lanes))
    to_left = jnp.where(col_id < patch, 1.0, 0.0).astype(BF16)
    to_right = jnp.where(col_id < patch, 0.0, 1.0).astype(BF16)
    each_half = jnp.where((row_id < patch) == (col_id < patch), 1.0, 0.0).astype(BF16)
    nothing = jnp.zeros((lanes, lanes), BF16)

    def prepare():
        for r in range(0, patch, block):
            part = slice(r, r + block)
            cs = jnp.zeros((block, lanes), F32)
            bw = jnp.zeros((block, lanes), F32)
            for c in range(0, full, lanes):
                columns = slice(c, c + lanes)
                plain = head[part, columns].astype(F32)
                scaled = (plain * (1.0 + mod[1:2, columns])).astype(BF16)
                wide[c // width, part, c % width : c % width + lanes] = scaled
                cs = cs + scaled.astype(F32)
                bw = bw + plain * mod[0:1, columns]
            sums_part[part, :], shift_part[part, :] = cs, bw

    def features(group):
        first = group[0] == 0
        product = dot_nt(hid[group[0]], wide[group[0]])
        for k in group[1:]:
            product = product + dot_nt(hid[k], wide[k])
        acc[...] = product if first else acc[...] + product
        for r in range(0, tokens, block):
            part = slice(r, r + block)
            centre = pilot[part, :]
            total = jnp.zeros((block, lanes), F32) if first else ssq[part, :]
            for k in group:
                for c in range(0, width, lanes):
                    value = hid[k, part, c : c + lanes].astype(F32) - centre
                    total = total + value * value
            ssq[part, :] = total

    def phase_mixed():
        product = dot_nt(cols[...], proj[...])
        centre = product[shard : shard + 1, 0:channels] * (1.0 / features_r)
        mixed[0:shard, :] = (
            product[0:shard, 0:channels] - product[0:shard, channels : channels + 1] * centre
        ).astype(BF16)

    def phase_gram():
        product = dot_nt(proj[...], proj[...]) * (1.0 / features_r)
        centre = product[0:channels, channels : channels + 1]
        gram = product[0:channels, 0:channels] - centre * product[channels : channels + 1, 0:channels]
        high = gram.astype(BF16)
        mixed[4 * shard : 4 * shard + channels, :] = high
        mixed[4 * shard + channels :, :] = (gram - high.astype(F32)).astype(BF16)

    def column_sums(values):
        pieces = []
        for value in values:
            high, rest = two_parts(value)
            low = (value - high.astype(F32) - rest.astype(F32)).astype(BF16)
            pieces += [jnp.concatenate([high, rest, low], axis=1)] * 2
        return dot_nt(jnp.ones((8, 3 * lanes), BF16), jnp.concatenate(pieces, axis=0))[0:1, :]

    def far(source, target, index, device):
        return pltpu.make_async_remote_copy(
            src_ref=source,
            dst_ref=target,
            send_sem=far_send.at[index],
            recv_sem=far_recv.at[index],
            device_id=device,
            device_id_type=MESH,
        )

    def share(index, source, target, device):
        moves = [
            far(
                mixed.at[pl.ds(source * shard, shard)],
                mixed.at[pl.ds(target * shard, shard)],
                index,
                device,
            ),
            far(vec.at[source], vec.at[target], index + 1, device),
        ]
        for move in moves:
            move.start()
        return moves

    load_mod.wait()
    load_head.wait()
    prepare()
    sums = column_sums([sums_part[...], shift_part[...]])
    head_sums, head_shift = sums[:, 0:lanes], sums[:, lanes:]
    hid_loads[0].wait()
    pilot[...] = jnp.broadcast_to(hid[0, :, 0:1].astype(F32), pilot.shape)
    groups = [[0]] + [list(range(k, min(k + 2, chunks))) for k in range(1, chunks, 2)]
    for group in groups:
        for k in group:
            if k > 0:
                hid_loads[k].wait()
        if group is groups[-1]:
            load_noisy.wait()
            token = lax.broadcasted_iota(jnp.int32, (TPF, 2 * TPF), 0)
            place = lane_at((TPF, 2 * TPF))
            pick = jnp.concatenate([place == token, place == token + TPF], axis=0)
            both = dot_nt(jnp.where(pick, 1.0, 0.0).astype(BF16), noisy[...])
            pair_rows = jnp.concatenate([both[0:TPF], both[TPF:]], axis=1)
            latents[...] = pair_rows
        features(group)
        if group is groups[1]:
            load_proj.wait()
            load_cols.wait()
            phase_mixed()
            load_vec.wait()
            vec[0] = jnp.broadcast_to(vec_in[...].astype(F32), vec.shape[1:])
            reached = len(reach) + jnp.where(has_before, 1, 0) + jnp.where(has_after, 1, 0)
            pl.semaphore_wait(barrier, reached)
            share_pair = share(2, 0, 1, pair)
            share_twin = share(4, 0, 2, twin)
    step_frac = jnp.full((1, lanes), timestep[0].astype(F32)) / 1000.0
    sigma = 5.0 * step_frac / (1.0 + 4.0 * step_frac)

    def phase_latents():
        one, two = acc[0:TPF, :], acc[TPF:, :]
        average = jnp.where(left, pltpu.roll(one, patch, 1), two) * (1.0 / full)
        product = jnp.where(left, one, pltpu.roll(two, patch, 1))
        off = average - jnp.where(left, pilot[0:TPF, :], pilot[TPF:, :])
        square = lane_sums([ssq[0:TPF, :], ssq[TPF:, :]], [to_left, to_right])
        var = jnp.maximum(square * (1.0 / full) - off * off, 0.0)
        scale = lax.rsqrt(var + EPSILON)
        mean[...] = average
        rstd[...] = scale
        velocity = scale * (product - average * head_sums)
        vel0[...] = velocity
        xown[...] = (latents[...] - sigma * (velocity + head_shift)).astype(BF16)

    phase_latents()

    move_x = far(xown, xhalo, 0, after)

    @pl.when(has_after)
    def _():
        move_x.start()

    phase_gram()
    for copy in load_conv + load_up:
        copy.wait()
    a0[...] = dot_nn(xown[...], conv[2 * patch :, :])

    @pl.when(has_before)
    def _():
        move_x.wait_recv()

    def phase_feat():
        a0[...] += dot_nn(xhalo[...], conv[0 : 2 * patch, :])
        for f in range(2):
            for r in range(0, TPF, block):
                value = a0[r : r + block, f * channels : (f + 1) * channels]
                feat[f * TPF + r : f * TPF + r + block, :] = silu(value).astype(BF16)

    phase_feat()

    def phase_upsample():
        for j in range(SUB):
            part = slice(j * channels, (j + 1) * channels)
            a1[:, part] = dot_nn(feat[...], up[:, part])
            for f in range(2):
                for p in range(REGIONS):
                    begin = f * TPF + p * span
                    pooled = jnp.sum(
                        silu(a1[begin : begin + span, part]), axis=0, keepdims=True
                    )
                    row = p * slots + f * SUB + j
                    emb32[row : row + 1, :] = pooled * (1.0 / span)

    phase_upsample()
    emb[...] = emb32[...].astype(BF16)

    order = list(range(slices - 1, -1, -1))
    line = list(range(slices))
    first_half, second_half = line[:2], line[2:]

    def send_emb(q, place, device):
        return pltpu.make_async_remote_copy(
            src_ref=emb,
            dst_ref=eall.at[place],
            send_sem=emb_send.at[q],
            recv_sem=emb_recv.at[place],
            device_id=device,
            device_id_type=MESH,
        )

    move_emb = {}
    for q, offset in ((3, -3), (2, 2), (1, -1), (0, 0)):
        place = lax.rem(q + turn(chip(offset)), slices)
        move_emb[q] = send_emb(q, place, other_core(offset))
        move_emb[q].start()

    for move in share_pair:
        move.wait_recv()
    share_on = share(6, 1, 3, twin)

    def phase_slopes():
        for f in range(2):
            for r in range(0, TPF, block):
                for j in range(SUB):
                    part = slice(j * channels, (j + 1) * channels)
                    where = slice(f * TPF + r, f * TPF + r + block)
                    a1[where, part] = silu_slope(a1[where, part])
                part = slice(f * channels, (f + 1) * channels)
                a0[r : r + block, part] = silu_slope(a0[r : r + block, part])

    phase_slopes()
    for move in share_twin + share_on:
        move.wait_recv()
    weight = jnp.concatenate([vec[q] for q in range(4)], axis=1)[0:1, :]
    slot = lax.rem(lax.broadcasted_iota(jnp.int32, (rows, 1), 0), slots) + ctx * slots
    present = jnp.where((slot == 0) | (slot >= SUB), 1.0, 0.0)
    row_scale = present * (-LOSS_WEIGHT / REGIONS / span)

    def row_of(d):
        return line.index(d) * rows

    def all_rows(group):
        return slice(row_of(group[0]), row_of(group[-1]) + rows)

    def reward(group):
        part = all_rows(group)
        both = 4 * shard
        terms[part, :] = dot_nt(
            jnp.concatenate([eall[d] for d in group], axis=0), mixed[...]
        )
        coeff = 0.7978845608028654
        for d in group:
            total = None
            for r in range(0, rows, block):
                where = slice(row_of(d) + r, row_of(d) + r + block)
                pulled = terms[where, both : both + channels] + terms[where, both + channels :]
                own_emb = eall[d, r : r + block, :].astype(F32)
                var = jnp.sum(pulled * own_emb, axis=1, keepdims=True)
                scale = lax.rsqrt(jnp.maximum(var, 0.0) + EPSILON)
                value = terms[where, :both] * scale
                square = value * value
                tangent = jnp.tanh(value * (coeff + (coeff * 0.044715) * square))
                half = 0.5 * (1.0 + tangent)
                slope = half + 0.5 * value * (1.0 - tangent * tangent) * (
                    coeff + (coeff * 3.0 * 0.044715) * square
                )
                slope = (weight * slope).astype(BF16)
                g[where, :] = slope
                along = jnp.sum(slope.astype(F32) * value, axis=1, keepdims=True)
                factor = scale * row_scale[r : r + block]
                factors[where, :] = jnp.broadcast_to(factor, (block, 128))
                terms[where, both : both + channels] = pulled * (factor * scale * along)
                points = value * half * weight
                for q in range(0, block, slots):
                    for c in range(0, both, 128):
                        piece = points[q : q + slots, c : c + 128]
                        total = piece if total is None else total + piece
            ssend[d] = total

    def gradient(group):
        part = all_rows(group)
        both = 4 * shard
        back = dot_nn(g[part, :], mixed[0:both, :])
        for d in group:
            where = slice(row_of(d), row_of(d) + rows)
            begin = row_of(d) - part.start
            dsend[d] = (
                back[begin : begin + rows] * factors[where, 0:1]
                - terms[where, both : both + channels]
            ).astype(BF16)

    def give_back(source, target, send_sem, recv_sem, p):
        q = lax.rem(p + slices - turn(z), slices)
        return pltpu.make_async_remote_copy(
            src_ref=source.at[p],
            dst_ref=target.at[q],
            send_sem=send_sem.at[p],
            recv_sem=recv_sem.at[q],
            device_id=other_core(-q),
            device_id_type=MESH,
        )

    def arrival(source, target, send_sem, recv_sem, q):
        return pltpu.make_async_remote_copy(
            src_ref=source.at[q],
            dst_ref=target.at[q],
            send_sem=send_sem.at[q],
            recv_sem=recv_sem.at[q],
            device_id=twin,
            device_id_type=MESH,
        )

    back_refs = (dsend, drecv, dem_send, dem_recv)
    score_refs = (ssend, srecv, sco_send, sco_recv)
    move_dem, move_sco = {}, {}

    def serve(group):
        for p in group:
            send_emb(0, p, twin).wait_recv()
        reward(group)
        gradient(group)
        for p in group:
            move_dem[p] = give_back(*back_refs, p)
            move_dem[p].start()

    serve(first_half)
    serve(second_half)
    for p in line:
        move_sco[p] = give_back(*score_refs, p)
        move_sco[p].start()

    for q in line:
        arrival(*back_refs, q).wait_recv()
    demb = drecv[0].astype(F32)
    for d in range(1, slices):
        demb = demb + drecv[d].astype(F32)
    emb32[...] = demb

    def phase_da0():
        for f in range(2):
            for j in range(SUB):
                part = slice(j * channels, (j + 1) * channels)
                spread = jnp.concatenate(
                    [
                        jnp.broadcast_to(
                            emb32[p * slots + f * SUB + j : p * slots + f * SUB + j + 1, :],
                            (span, channels),
                        )
                        for p in range(REGIONS)
                    ],
                    axis=0,
                )
                da1[f * TPF : (f + 1) * TPF, part] = (
                    spread * a1[f * TPF : (f + 1) * TPF, part]
                ).astype(BF16)
            dfeat = dot_nt(da1[f * TPF : (f + 1) * TPF, :], up[...])
            part = slice(f * channels, (f + 1) * channels)
            da0[:, part] = (dfeat * a0[:, part]).astype(BF16)

    phase_da0()

    def phase_hsend():
        hsend[...] = dot_nt(da0[...], conv[0 : 2 * patch, :]).astype(BF16)

    phase_hsend()
    move_h = far(hsend, hrecv, 1, before)

    @pl.when(has_before)
    def _():
        move_h.start()

    own = dot_nt(da0[...], conv[2 * patch :, :])

    for d in order:
        arrival(*score_refs, d).wait_recv()
    total = srecv[0]
    for d in range(1, slices):
        total = total + srecv[d]
    total = jnp.sum(total, axis=1, keepdims=True) / REGIONS
    index = lax.broadcasted_iota(jnp.int32, (slots, 128), 0)
    where = index + ctx * slots
    keep = ((where == 0) | (where >= SUB)) & (index == lane_at((slots, 128)))
    reward_out[...] = jnp.sum(jnp.where(keep, total, 0.0), axis=0, keepdims=True)

    @pl.when(has_after)
    def _():
        move_h.wait_recv()

    def phase_final():
        grad = (-sigma) * (own + hrecv[...].astype(F32))
        lean = (rstd[...] * grad).astype(BF16).astype(F32)
        means = lane_sums(
            [lean * head_sums, lean * vel0[...]],
            [
                jnp.concatenate([each_half, nothing], axis=1),
                jnp.concatenate([nothing, each_half], axis=1),
            ],
        ) * (1.0 / full)
        one = means[:, 0:lanes]
        slope = rstd[...] * means[:, lanes:]
        offset = slope * mean[...] - one
        high = offset.astype(BF16).astype(F32)
        middle = (offset - high).astype(BF16).astype(F32)
        low = offset - high - middle
        nth = lax.rem(lane_at((TPF, lanes)), patch)
        tail = jnp.where(nth == 0, high, jnp.where(nth == 1, middle, low))
        tail = jnp.where(nth < 3, tail, 0.0)
        other = pltpu.roll(slope, patch, 1)
        lhs_out[0:TPF, :] = jnp.where(left, lean, pltpu.roll(tail, patch, 1)).astype(BF16)
        lhs_out[TPF:, :] = jnp.where(left, pltpu.roll(lean, patch, 1), tail).astype(BF16)
        coef_out[0:TPF, :] = jnp.where(left, slope, other)
        coef_out[TPF:, :] = jnp.where(left, other, slope)

    phase_final()

    @pl.when(has_after)
    def _():
        move_x.wait_send()

    @pl.when(has_before)
    def _():
        move_h.wait_send()

    for move in share_pair + share_twin + share_on:
        move.wait_send()
    for d in order:
        move_emb[d].wait_send()
        move_dem[d].wait_send()
        move_sco[d].wait_send()


def tail_kernel(hid, wide, lhs, coef, rewards, grad, reward_out, held, held_rewards, sem):
    chunks, tokens, width = hid.shape
    lanes = coef.shape[1]
    piece = width // 2
    block = 16
    held_rewards[...] = rewards[:, : held_rewards.shape[1]]
    copies = [pltpu.make_async_copy(held_rewards, reward_out, sem.at[0])]
    copies[0].start()
    for k in range(chunks):
        for begin in range(0, width, piece):
            product = dot_nn(lhs[...], wide[k, :, begin : begin + piece])
            first = k * width + begin
            for r in range(0, tokens, block):
                part = slice(r, r + block)
                slope = coef[part, :]
                for c in range(0, piece, lanes):
                    value = hid[k, part, begin + c : begin + c + lanes].astype(F32)
                    held[part, first + c : first + c + lanes] = (
                        product[part, c : c + lanes] - value * slope
                    ).astype(BF16)
            columns = pl.ds(first, piece)
            copy = pltpu.make_async_copy(
                held.at[:, columns], grad.at[:, columns], sem.at[len(copies)]
            )
            copy.start()
            copies.append(copy)
    for copy in copies:
        copy.wait()


def per_device(
    hidden,
    modulation,
    head_weight,
    noisy,
    timestep,
    conv_weight,
    up_weight,
    patch_proj,
    fc1,
    reward_vec,
):
    states = hidden[0]
    tokens, full = states.shape
    patch = head_weight.shape[0]
    channels = up_weight.shape[1]
    features_r, shard = fc1.shape
    slices = 4
    rows = 2 * SUB * REGIONS
    slots = 2 * SUB
    lanes = 2 * patch
    width = 1024
    chunks = full // width
    vmem = pltpu.VMEM

    scratch = [
        vmem((2, full), F32),
        vmem((patch, full), BF16),
        vmem((patch, tokens), BF16),
        vmem((4 * patch, 2 * channels), BF16),
        vmem((channels, SUB * channels), BF16),
        vmem((channels + 16, features_r), BF16),
        vmem((shard + 16, features_r), BF16),
        vmem((4 * shard + 2 * channels, channels), BF16),
        vmem((4, 8, shard), F32),
        vmem((1, shard), BF16),
        vmem((tokens, lanes), F32),
        vmem((tokens, lanes), F32),
        vmem((tokens, lanes), F32),
        vmem((patch, lanes), F32),
        vmem((patch, lanes), F32),
        vmem((TPF, lanes), F32),
        vmem((TPF, lanes), F32),
        vmem((TPF, lanes), F32),
        vmem((TPF, lanes), F32),
        vmem((TPF, lanes), BF16),
        vmem((TPF, lanes), BF16),
        vmem((TPF, 2 * channels), F32),
        vmem((tokens, channels), BF16),
        vmem((tokens, SUB * channels), F32),
        vmem((rows, channels), F32),
        vmem((rows, channels), BF16),
        vmem((slices, rows, channels), BF16),
        vmem((slices * rows, 4 * shard + 2 * channels), F32),
        vmem((slices * rows, 128), F32),
        vmem((slices * rows, 4 * shard), BF16),
        vmem((slices, rows, channels), BF16),
        vmem((slices, rows, channels), BF16),
        vmem((slices, slots, 128), F32),
        vmem((slices, slots, 128), F32),
        vmem((tokens, SUB * channels), BF16),
        vmem((TPF, 2 * channels), BF16),
        vmem((TPF, lanes), BF16),
        vmem((TPF, lanes), BF16),
        pltpu.SemaphoreType.DMA((chunks,)),
        pltpu.SemaphoreType.DMA((20,)),
        pltpu.SemaphoreType.DMA((8,)),
        pltpu.SemaphoreType.DMA((8,)),
        pltpu.SemaphoreType.DMA((slices,)),
        pltpu.SemaphoreType.DMA((slices,)),
        pltpu.SemaphoreType.DMA((slices,)),
        pltpu.SemaphoreType.DMA((slices,)),
        pltpu.SemaphoreType.DMA((slices,)),
        pltpu.SemaphoreType.DMA((slices,)),
    ]
    in_hbm = pl.BlockSpec(memory_space=pltpu.HBM)
    local = pl.BlockSpec(memory_space=pltpu.VMEM)
    hid, wide, lhs, coef, rewards = pl.pallas_call(
        main_kernel,
        out_shape=(
            vmem((chunks, tokens, width), BF16),
            vmem((chunks, lanes, width), BF16),
            vmem((tokens, lanes), BF16),
            vmem((tokens, lanes), F32),
            vmem((1, 128), F32),
        ),
        in_specs=[pl.BlockSpec(memory_space=pltpu.SMEM)] + [in_hbm] * 9,
        out_specs=(local,) * 5,
        scratch_shapes=scratch,
        compiler_params=pltpu.CompilerParams(
            collective_id=0, has_side_effects=True, vmem_limit_bytes=36 * 1024 * 1024
        ),
        name="reward_step",
    )(
        timestep,
        *(
            pltpu.with_memory_space_constraint(value, pltpu.HBM)
            for value in (
                states,
                modulation,
                head_weight,
                noisy[0].T,
                conv_weight,
                up_weight,
                patch_proj,
                fc1.T,
                reward_vec,
            )
        ),
    )
    grad, reward = pl.pallas_call(
        tail_kernel,
        out_shape=(
            jax.ShapeDtypeStruct((tokens, full), BF16),
            jax.ShapeDtypeStruct((1, slots), F32),
        ),
        in_specs=[local] * 5,
        out_specs=(in_hbm, in_hbm),
        scratch_shapes=[
            vmem((tokens, full), BF16),
            vmem((1, slots), F32),
            pltpu.SemaphoreType.DMA((2 * chunks + 1,)),
        ],
        compiler_params=pltpu.CompilerParams(vmem_limit_bytes=20 * 1024 * 1024),
        name="hidden_gradient",
    )(hid, wide, lhs, coef, rewards)
    return (grad[None], reward)


def solution(mesh):
    return jax.shard_map(
        per_device,
        mesh=mesh,
        in_specs=(
            P("fsdp", "ctx", None),
            P(),
            P(),
            P("fsdp", "ctx", None),
            P(),
            P(),
            P(),
            P(),
            P(None, "fsdp"),
            P(None, "fsdp"),
        ),
        out_specs=(P("fsdp", "ctx", None), P("fsdp", "ctx")),
        check_vma=False,
    )
```
